32 devices in a mesh: seq: 16 (over z, y, x), head: 2 (over core).
Axes of the slice: x: 2, y: 2, z: 4, core: 2. Of those that a mesh axis runs over, the one named last changes fastest.
Arguments:
- queries: bfloat16 [16, 128, 576], P(None, 'head'), may hold values from -24 to 24
- cache: bfloat16 [16, 2048, 576], P(None, 'seq'), may hold values from -4 to 4
- block_ids: int32 [16, 32], replicated, may hold values from 0 to 31, as said below
- lengths: int32 [16], replicated, may hold values from 2048 to 2048, as said below
- value_up: bfloat16 [128, 512, 128], P('head'), may hold values from -2 to 2
- out_proj: bfloat16 [16384, 7168], P('head', 'seq'), may hold values from -0.046875 to 0.046875
Outputs:
- mixed: bfloat16 [16, 7168], P(None, 'seq')
The draws below stay inside these ranges and needn't reach their ends.
Inputs may be any that keep to these rules, and one draw needn't show every extreme that they name: `block_ids`: each row's block numbers are distinct, each below ceil(lengths / 64), and include the row's last filled block. `lengths`: some row is full in every draw.
All inputs are finite; a program needn't handle non-finite values.
Results may differ from the reference program's by a relative error of at most 0.019.
Values may be sent and summed in bfloat16 or wider, within the bound.
A program may use at most 64 MiB of HBM per device.

```python
import jax
import jax.numpy as jnp
from jax import lax

HEADS = 128
LATENT = 512
VDIM = 128
D = 7168
BLOCK = 64
BLOCKS = 32
ROWS = 16
KV = 576
LEN = 2048
NBLK = 32
N_HEAD = 2


def shared_lengths(key):
    first = jax.random.fold_in(key, 771)
    second = jax.random.fold_in(key, 772)
    drawn = jax.random.randint(first, (ROWS,), BLOCKS * BLOCK, LEN + 1, dtype=jnp.int32)
    full_row = jax.random.randint(second, (), 0, ROWS, dtype=jnp.int32)
    return jnp.where(jnp.arange(ROWS, dtype=jnp.int32) == full_row, jnp.int32(LEN), drawn)


def draw_queries(key, part):
    key = jax.random.fold_in(key, 1)
    values = jnp.clip(1.5 * jax.random.normal(key, (ROWS, HEADS, KV), jnp.float32), -9.0, 9.0)
    return values.astype(jnp.bfloat16)


def draw_cache(key, part):
    key = jax.random.fold_in(key, 2)
    values = jnp.clip(jax.random.normal(key, (ROWS, LEN, KV), jnp.float32), -4.0, 4.0)
    return values.astype(jnp.bfloat16)


def draw_lengths(key, part):
    return shared_lengths(key)


def draw_block_ids(key, part):
    lens = shared_lengths(key)
    key = jax.random.fold_in(key, 3)
    filled = (lens + BLOCK - 1) // BLOCK
    number = jnp.arange(NBLK, dtype=jnp.int32)[None, :]
    noise = jax.random.randint(key, (ROWS, NBLK), 0, 4096, dtype=jnp.int32)
    score = noise * NBLK + number
    score = jnp.where(number >= filled[:, None] - 8, score + 4096 * NBLK, score)
    score = jnp.where(number == filled[:, None] - 1, jnp.int32(2 ** 30), score)
    score = jnp.where(number >= filled[:, None], jnp.int32(-1), score)
    return lax.top_k(score, BLOCKS)[1].astype(jnp.int32)


def shard_levels(own_key, dims, shards, low, top_value):
    gain, own = 1.0, jax.random.fold_in(own_key, 6)
    for axis_at, blocks in shards:
        draws = jnp.exp(jax.random.uniform(jax.random.fold_in(own, axis_at), (blocks,), jnp.float32, low / len(shards), top_value / len(shards)))
        gain = gain * jnp.repeat(draws, dims[axis_at] // blocks).reshape([-1 if axis == axis_at else 1 for axis in range(len(dims))])
    return gain


def centred(key, shape, scale, bound, shards=(), held_as=jnp.bfloat16):
    result = jax.random.normal(key, shape, jnp.float32) * scale
    if len(shards) > 0:
        result = shard_levels(key, shape, shards, -0.22, 0.18) * result
    return jnp.clip(result, min=-bound, max=bound).astype(held_as)


def setup_inputs(seed: int = 0) -> dict:
    splits = jax.random.split(jax.random.key(seed), 7)
    return {
        "queries": draw_queries(jax.random.fold_in(splits[6], 71), 0),
        "cache": draw_cache(jax.random.fold_in(splits[6], 71), 0),
        "block_ids": draw_block_ids(jax.random.fold_in(splits[6], 71), 0),
        "lengths": draw_lengths(jax.random.fold_in(splits[6], 71), 0),
        "value_up": centred(splits[4], (HEADS, LATENT, VDIM), (max(LATENT // 64, 1)) ** -0.5, 2.0, ((0, 2),)),
        "out_proj": centred(splits[5], (HEADS * VDIM, D), (HEADS * VDIM) ** -0.5, 0.046875, ((0, 2), (1, 16))),
    }


softmax_scale = 192.0 ** -0.5


def reference(queries, cache, block_ids, lengths, value_up, out_proj):
    offsets = jnp.arange(BLOCK, dtype=jnp.int32)
    position = (block_ids[:, :, None] * BLOCK + offsets[None, None, :]).reshape(ROWS, BLOCKS * BLOCK).astype(jnp.int32)
    row_index = jnp.arange(ROWS, dtype=jnp.int32)[:, None]
    picked = cache[row_index, position]
    live = position < lengths[:, None]
    scores = jnp.einsum("rhc,rsc->rhs", queries.astype(jnp.float32), picked.astype(jnp.float32)) * softmax_scale
    masked = jnp.where(live[:, None, :], scores, -jnp.inf)
    top = jnp.max(masked, axis=-1, keepdims=True)
    expo = jnp.where(live[:, None, :], jnp.exp(masked - top), jnp.float32(0.0))
    total = jnp.sum(expo, axis=-1)
    weights = expo.astype(jnp.bfloat16)
    summed = jnp.einsum("rhs,rsc->rhc", weights.astype(jnp.float32), picked[:, :, :LATENT].astype(jnp.float32))
    context = summed / total[:, :, None]
    heads_out = jnp.einsum("rhc,hcv->rhv", context, value_up.astype(jnp.float32), precision=lax.Precision.HIGHEST).astype(jnp.bfloat16)
    group_cols = (HEADS // N_HEAD) * VDIM
    grouped = heads_out.reshape(ROWS, N_HEAD, group_cols).astype(jnp.float32)
    proj_groups = out_proj.reshape(N_HEAD, group_cols, D).astype(jnp.float32)
    group_out = jnp.einsum("rgc,gcd->grd", grouped, proj_groups, precision=lax.Precision.HIGHEST).astype(jnp.bfloat16)
    return jnp.sum(group_out.astype(jnp.float32), axis=0).astype(jnp.bfloat16)
```

```python
import functools

import jax
import jax.numpy as jnp
from jax import lax
from jax.experimental import pallas as pl
from jax.experimental.pallas import tpu as pltpu
from jax.sharding import PartitionSpec as P

BLOCK = 64
DEAD = -1e30
MESH = pl.DeviceIdType.MESH


softmax_scale = 192.0 ** (-0.5)


def kernel(
    n,
    n_head,
    lengths_ref,
    ids_ref,
    q_hbm,
    k_hbm,
    v_hbm,
    w_hbm,
    out_ref,
    q,
    k,
    v,
    w,
    scores,
    summed,
    stat_out,
    stat_in,
    spread,
    part_out,
    part_in,
    flat,
    group,
    local_sem,
    v_sem,
    w_sem,
    stat_send,
    stat_recv,
    part_send,
    part_recv,
    flat_send,
    flat_recv,
    group_send,
    group_recv,
):
    rows, heads, width = q.shape
    span = k.shape[2]
    latent, vdim = v.shape[1:]
    own = heads // n
    tiles = latent // 128
    piece = own * vdim
    me = lax.axis_index("seq")
    my_head = lax.axis_index("head")

    def v_copy(t):
        part = pl.ds(t * own, own)
        return pltpu.make_async_copy(v_hbm.at[part], v.at[part], v_sem.at[t])

    def w_copy(t):
        part = pl.ds(pl.multiple_of(t * piece, piece), piece)
        return pltpu.make_async_copy(w_hbm.at[:, part], w.at[t], w_sem.at[t])

    q_copy = pltpu.make_async_copy(q_hbm, q, local_sem.at[0])
    k_copy = pltpu.make_async_copy(k_hbm, k, local_sem.at[1])
    q_copy.start()
    k_copy.start()

    barrier = pltpu.get_barrier_semaphore()

    @pl.loop(1, n)
    def _(i):
        pl.semaphore_signal(
            barrier, inc=1, device_id={"seq": lax.rem(me + i, n)}, device_id_type=MESH
        )

    for j in range(1, n_head):
        pl.semaphore_signal(
            barrier, inc=1, device_id={"head": lax.rem(my_head + j, n_head)}, device_id_type=MESH
        )

    @pl.loop(1, n + 1)
    def _(i):
        v_copy(lax.rem(me + i, n)).start()

    @pl.loop(0, n)
    def _(i):
        w_copy(lax.rem(me + i, n)).start()

    lane = lax.broadcasted_iota(jnp.int32, (rows, span), 1)
    line = lax.broadcasted_iota(jnp.int32, (rows, span), 0)
    first = me * span
    ids = ids_ref[...]
    chosen = jnp.zeros((rows, span), jnp.int32)
    for b in range(span // BLOCK):
        hit = jnp.max((ids == first // BLOCK + b).astype(jnp.int32), axis=1, keepdims=True)
        chosen = jnp.where(lane // BLOCK == b, hit, chosen)
    filled = jnp.zeros((rows, span), jnp.int32)
    for r in range(rows):
        filled = jnp.where(line == r, lengths_ref[r], filled)
    live = jnp.where(first + lane < filled, chosen, 0).astype(jnp.float32)

    q_copy.wait()
    k_copy.wait()
    for r in range(rows):
        s = jnp.dot(q[r], k[r], preferred_element_type=jnp.float32) * softmax_scale
        scores[r] = jnp.where(live[r : r + 1] > 0.0, s, DEAD)
    stats = jnp.zeros((heads, 128), jnp.float32)
    stat_lane = lax.broadcasted_iota(jnp.int32, (heads, 128), 1)
    for r in range(rows):
        s = scores[r]
        top = jnp.max(s, axis=1, keepdims=True)
        expo = jnp.where(live[r : r + 1] > 0.0, jnp.exp(s - top), 0.0)
        total = jnp.sum(expo, axis=1, keepdims=True)
        some = total > 0.0
        total = jnp.where(some, total, 1.0)
        stats = jnp.where(stat_lane == r, jnp.where(some, top + jnp.log(total), DEAD), stats)
        out = lax.dot_general(
            expo.astype(jnp.bfloat16),
            k[r, :latent, :],
            (((1,), (1,)), ((), ())),
            preferred_element_type=jnp.float32,
        )
        out = out * (1.0 / total)
        for c in range(tiles):
            summed[c, r * heads : (r + 1) * heads, :] = out[:, c * 128 : (c + 1) * 128]
    for t in range(n):
        stat_out[t] = stats[t * own : (t + 1) * own]

    pl.semaphore_wait(barrier, n - 1 + n_head - 1)

    def stat_copy(t, slot):
        return pltpu.make_async_remote_copy(
            src_ref=stat_out.at[t],
            dst_ref=stat_in.at[slot],
            send_sem=stat_send.at[t],
            recv_sem=stat_recv.at[slot],
            device_id={"seq": t},
            device_id_type=MESH,
        )

    def part_copy(t, slot):
        return pltpu.make_async_remote_copy(
            src_ref=part_out.at[t],
            dst_ref=part_in.at[slot],
            send_sem=part_send.at[t],
            recv_sem=part_recv.at[slot],
            device_id={"seq": t},
            device_id_type=MESH,
        )

    def flat_copy(t, slot):
        return pltpu.make_async_remote_copy(
            src_ref=flat.at[slot],
            dst_ref=flat.at[slot],
            send_sem=flat_send.at[t],
            recv_sem=flat_recv.at[slot],
            device_id={"seq": t},
            device_id_type=MESH,
        )

    @pl.loop(1, n)
    def _(i):
        stat_copy(lax.rem(me + i, n), me).start()

    def project(t, dst):
        v_copy(t).wait()
        for j in range(own):
            h = t * own + j
            x = jnp.concatenate(
                [summed[c, pl.ds(h, rows, stride=heads), :] for c in range(tiles)], axis=1
            )
            y = jnp.dot(x.astype(jnp.bfloat16), v[h], preferred_element_type=jnp.float32)
            dst[j] = y.astype(jnp.bfloat16)

    @pl.loop(1, n)
    def _(i):
        t = lax.rem(me + i, n)
        project(t, part_out.at[t])
        part_copy(t, me).start()

    project(me, part_in.at[me])
    stat_in[me] = stat_out[me]

    @pl.loop(1, n)
    def _(i):
        stat_copy(me, lax.rem(me + n - i, n)).wait_recv()

    got = [stat_in[d] for d in range(n)]
    best = functools.reduce(jnp.maximum, got)
    got = [jnp.exp(g - best) for g in got]
    scale = 1.0 / functools.reduce(jnp.add, got)
    for d in range(n):
        spread[d * own : (d + 1) * own, :] = got[d] * scale
    share = jnp.transpose(spread[...])[:rows]

    @pl.loop(1, n)
    def _(i):
        part_copy(me, lax.rem(me + n - i, n)).wait_recv()

    for j in range(own):
        y = jnp.zeros((rows, vdim), jnp.float32)
        for d in range(n):
            at = d * own + j
            y = y + share[:, at : at + 1] * part_in[d, j].astype(jnp.float32)
        flat[me, :, j * vdim : (j + 1) * vdim] = y.astype(jnp.bfloat16)

    @pl.loop(1, n)
    def _(i):
        flat_copy(lax.rem(me + i, n), me).start()

    def multiply(t):
        w_copy(t).wait()
        return lax.dot_general(
            flat[t], w[t], (((1,), (1,)), ((), ())), preferred_element_type=jnp.float32
        )

    def step(i, total):
        t = lax.rem(me + n - i, n)
        flat_copy(me, t).wait_recv()
        return total + multiply(t)

    total = lax.fori_loop(1, n, step, multiply(me))
    group[my_head] = total.astype(jnp.bfloat16)

    def group_copy(to, slot):
        return pltpu.make_async_remote_copy(
            src_ref=group.at[slot],
            dst_ref=group.at[slot],
            send_sem=group_send.at[to],
            recv_sem=group_recv.at[slot],
            device_id={"head": to},
            device_id_type=MESH,
        )

    for j in range(1, n_head):
        group_copy(lax.rem(my_head + j, n_head), my_head).start()
    for j in range(1, n_head):
        group_copy(my_head, lax.rem(my_head + j, n_head)).wait_recv()
    mixed = group[0].astype(jnp.float32)
    for g in range(1, n_head):
        mixed = mixed + group[g].astype(jnp.float32)
    out_ref[...] = mixed.astype(jnp.bfloat16)

    @pl.loop(1, n)
    def _(i):
        t = lax.rem(me + i, n)
        stat_copy(t, me).wait_send()
        part_copy(t, me).wait_send()
        flat_copy(t, me).wait_send()

    for j in range(1, n_head):
        group_copy(lax.rem(my_head + j, n_head), my_head).wait_send()


def fused(n, n_head, queries, cache, block_ids, lengths, value_up, out_proj):
    rows, heads, width = queries.shape
    span = cache.shape[1]
    latent, vdim = value_up.shape[1:]
    columns = out_proj.shape[1]
    own = heads // n
    dma = pltpu.SemaphoreType.DMA
    any_space = pl.BlockSpec(memory_space=pl.ANY)
    return pl.pallas_call(
        functools.partial(kernel, n, n_head),
        out_shape=jax.ShapeDtypeStruct((rows, columns), jnp.bfloat16),
        in_specs=[
            pl.BlockSpec(memory_space=pltpu.SMEM),
            pl.BlockSpec(memory_space=pltpu.VMEM),
            any_space,
            any_space,
            any_space,
            any_space,
        ],
        out_specs=pl.BlockSpec(memory_space=pltpu.VMEM),
        scratch_shapes=[
            pltpu.VMEM((rows, heads, width), jnp.bfloat16),
            pltpu.VMEM((rows, width, span), jnp.bfloat16),
            pltpu.VMEM((heads, latent, vdim), jnp.bfloat16),
            pltpu.VMEM((n, columns, own * vdim), jnp.bfloat16),
            pltpu.VMEM((rows, heads, span), jnp.float32),
            pltpu.VMEM((latent // 128, rows * heads, 128), jnp.float32),
            pltpu.VMEM((n, own, 128), jnp.float32),
            pltpu.VMEM((n, own, 128), jnp.float32),
            pltpu.VMEM((heads, 128), jnp.float32),
            pltpu.VMEM((n, own, rows, vdim), jnp.bfloat16),
            pltpu.VMEM((n, own, rows, vdim), jnp.bfloat16),
            pltpu.VMEM((n, rows, own * vdim), jnp.bfloat16),
            pltpu.VMEM((n_head, rows, columns), jnp.bfloat16),
            dma((2,)),
            dma((n,)),
            dma((n,)),
            dma((n,)),
            dma((n,)),
            dma((n,)),
            dma((n,)),
            dma((n,)),
            dma((n,)),
            dma((n_head,)),
            dma((n_head,)),
        ],
        compiler_params=pltpu.CompilerParams(
            collective_id=0, has_side_effects=True, vmem_limit_bytes=60 * 2**20
        ),
    )(
        lengths,
        block_ids,
        queries,
        jnp.transpose(cache, (0, 2, 1)),
        value_up,
        jnp.transpose(out_proj),
    )


def spread_body(queries, cache, block_ids, lengths, value_up, out_proj):
    rows, span, width = cache.shape
    latent = value_up.shape[1]
    first = lax.axis_index("seq") * span
    position = first + jnp.arange(span, dtype=jnp.int32)
    chosen = jnp.any(block_ids[:, :, None] == (position // BLOCK)[None, None, :], axis=1)
    live = chosen & (position[None, :] < lengths[:, None])
    scores = (
        jnp.einsum("rhc,rsc->rhs", queries, cache, preferred_element_type=jnp.float32)
        * softmax_scale
    )
    masked = jnp.where(live[:, None, :], scores, -jnp.inf)
    local_top = jnp.max(masked, axis=-1)
    top = lax.pmax(local_top, "seq")
    expo = jnp.where(live[:, None, :], jnp.exp(masked - top[:, :, None]), jnp.float32(0.0))
    local_total = jnp.sum(expo, axis=-1)
    weights = expo.astype(jnp.bfloat16)
    summed = jnp.einsum(
        "rhs,rsc->rhc", weights, cache[:, :, :latent], preferred_element_type=jnp.float32
    )
    upward = value_up.astype(jnp.float32)
    total, summed_all = lax.psum((local_total, summed), "seq")
    context = summed_all / total[:, :, None]
    heads_out = jnp.einsum("rhc,hcv->rhv", context, upward, precision=lax.Precision.HIGHEST)
    flat = heads_out.astype(jnp.bfloat16).reshape(rows, -1)
    partial_out = jnp.dot(flat, out_proj, preferred_element_type=jnp.float32)
    return lax.psum(partial_out.astype(jnp.bfloat16), "head")


def body(n, n_head, *args):
    heads, span = args[0].shape[1], args[1].shape[1]
    if heads % n or span % BLOCK or span % 128:
        return spread_body(*args)
    return fused(n, n_head, *args)


def solution(mesh):
    return jax.shard_map(
        functools.partial(body, mesh.shape["seq"], mesh.shape["head"]),
        mesh=mesh,
        in_specs=(
            P(None, "head", None),
            P(None, "seq", None),
            P(),
            P(),
            P("head", None, None),
            P("head", "seq"),
        ),
        out_specs=P(None, "seq"),
        check_vma=False,
    )
```

```python
import functools

import jax
import jax.numpy as jnp
from jax import lax
from jax.experimental import pallas as pl
from jax.experimental.pallas import tpu as pltpu
from jax.sharding import PartitionSpec as P

BLOCK = 64
DEAD = -1e30
GROUPS = 4
MESH = pl.DeviceIdType.MESH


softmax_scale = 192.0 ** (-0.5)


def kernel(
    n,
    n_head,
    lengths_ref,
    ids_ref,
    q_hbm,
    k_hbm,
    v_hbm,
    w_hbm,
    out_ref,
    q,
    k,
    v,
    w,
    scores,
    summed,
    stat_out,
    stat_in,
    spread,
    part_out,
    part_in,
    flat,
    group,
    local_sem,
    v_sem,
    w_sem,
    stat_send,
    stat_recv,
    part_send,
    part_recv,
    flat_send,
    flat_recv,
    group_send,
    group_recv,
):
    rows, heads, width = q.shape
    span = k.shape[2]
    latent, vdim = v.shape[1:]
    own = heads // n
    tiles = latent // 128
    piece = own * vdim
    me = lax.axis_index("seq")
    my_head = lax.axis_index("head")

    def v_copy(t):
        part = pl.ds(t * own, own)
        return pltpu.make_async_copy(v_hbm.at[part], v.at[part], v_sem.at[t])

    def w_copy(t):
        part = pl.ds(pl.multiple_of(t * piece, piece), piece)
        return pltpu.make_async_copy(w_hbm.at[:, part], w.at[t], w_sem.at[t])

    def first_copies(g):
        part = pl.ds(g * (rows // GROUPS), rows // GROUPS)
        return (
            pltpu.make_async_copy(q_hbm.at[part], q.at[part], local_sem.at[0, g]),
            pltpu.make_async_copy(k_hbm.at[part], k.at[part], local_sem.at[1, g]),
        )

    for g in range(GROUPS):
        for copy in first_copies(g):
            copy.start()

    half = n // 2
    side = me // half
    place = lax.rem(me, half)
    mirror = (1 - side) * half + place

    def near(i):
        return side * half + lax.rem(place + i, half)

    def far(i):
        return (1 - side) * half + lax.rem(place + i, half)

    barrier = pltpu.get_barrier_semaphore()

    @pl.loop(1, n)
    def _(i):
        pl.semaphore_signal(
            barrier, inc=1, device_id={"seq": lax.rem(me + i, n)}, device_id_type=MESH
        )

    for j in range(1, n_head):
        pl.semaphore_signal(
            barrier, inc=1, device_id={"head": lax.rem(my_head + j, n_head)}, device_id_type=MESH
        )

    lane = lax.broadcasted_iota(jnp.int32, (rows, span), 1)
    line = lax.broadcasted_iota(jnp.int32, (rows, span), 0)
    first = me * span
    ids = ids_ref[...]
    chosen = jnp.zeros((rows, span), jnp.int32)
    for b in range(span // BLOCK):
        hit = jnp.max((ids == first // BLOCK + b).astype(jnp.int32), axis=1, keepdims=True)
        chosen = jnp.where(lane // BLOCK == b, hit, chosen)
    filled = jnp.zeros((rows, span), jnp.int32)
    for r in range(rows):
        filled = jnp.where(line == r, lengths_ref[r], filled)
    live = jnp.where(first + lane < filled, chosen, 0).astype(jnp.float32)

    for r in range(rows):
        if r % (rows // GROUPS) == 0:
            for copy in first_copies(r // (rows // GROUPS)):
                copy.wait()
        s = jnp.dot(q[r], k[r], preferred_element_type=jnp.float32) * softmax_scale
        scores[r] = jnp.where(live[r : r + 1] > 0.0, s, DEAD)

    @pl.loop(0, half)
    def _(i):
        v_copy(far(i)).start()

    @pl.loop(1, half + 1)
    def _(i):
        v_copy(near(i)).start()

    stats = jnp.zeros((heads, 128), jnp.float32)
    stat_lane = lax.broadcasted_iota(jnp.int32, (heads, 128), 1)
    for r in range(rows):
        s = scores[r]
        top = jnp.max(s, axis=1, keepdims=True)
        expo = jnp.where(live[r : r + 1] > 0.0, jnp.exp(s - top), 0.0)
        total = jnp.sum(expo, axis=1, keepdims=True)
        some = total > 0.0
        total = jnp.where(some, total, 1.0)
        stats = jnp.where(stat_lane == r, jnp.where(some, top + jnp.log(total), DEAD), stats)
        out = lax.dot_general(
            expo.astype(jnp.bfloat16),
            k[r, :latent, :],
            (((1,), (1,)), ((), ())),
            preferred_element_type=jnp.float32,
        )
        out = out * (1.0 / total)
        for c in range(tiles):
            summed[c, r * heads : (r + 1) * heads, :] = out[:, c * 128 : (c + 1) * 128]
    for t in range(n):
        stat_out[t] = stats[t * own : (t + 1) * own]

    pl.semaphore_wait(barrier, n - 1 + n_head - 1)

    def stat_copy(t, slot):
        return pltpu.make_async_remote_copy(
            src_ref=stat_out.at[t],
            dst_ref=stat_in.at[slot],
            send_sem=stat_send.at[t],
            recv_sem=stat_recv.at[slot],
            device_id={"seq": t},
            device_id_type=MESH,
        )

    def part_copy(t, slot):
        return pltpu.make_async_remote_copy(
            src_ref=part_out.at[t],
            dst_ref=part_in.at[slot],
            send_sem=part_send.at[t],
            recv_sem=part_recv.at[slot],
            device_id={"seq": t},
            device_id_type=MESH,
        )

    def flat_copy(t, slot, sem):
        return pltpu.make_async_remote_copy(
            src_ref=flat.at[slot],
            dst_ref=flat.at[slot],
            send_sem=flat_send.at[sem],
            recv_sem=flat_recv.at[slot],
            device_id={"seq": t},
            device_id_type=MESH,
        )

    @pl.loop(1, n)
    def _(i):
        stat_copy(lax.rem(me + i, n), me).start()

    @pl.loop(0, half)
    def _(i):
        w_copy(near(i)).start()

    @pl.loop(0, half)
    def _(i):
        w_copy(far(i)).start()

    def project(t, dst):
        for j in range(own):
            h = t * own + j
            x = jnp.concatenate(
                [summed[c, pl.ds(h, rows, stride=heads), :] for c in range(tiles)], axis=1
            )
            y = jnp.dot(x.astype(jnp.bfloat16), v[h], preferred_element_type=jnp.float32)
            dst[j] = y.astype(jnp.bfloat16)

    def project_pair(t0, t1):
        v_copy(t0).wait()
        v_copy(t1).wait()
        project(t0, part_out.at[t0])
        project(t1, part_out.at[t1])
        part_copy(t0, me).start()
        part_copy(t1, me).start()

    @pl.loop(0, half // 2)
    def _(i):
        project_pair(far(2 * i), far(2 * i + 1))

    @pl.loop(0, half // 2 - 1)
    def _(i):
        project_pair(near(2 * i + 1), near(2 * i + 2))

    last = near(half - 1)
    v_copy(last).wait()
    v_copy(me).wait()
    project(last, part_out.at[last])
    part_copy(last, me).start()
    project(me, part_in.at[me])
    stat_in[me] = stat_out[me]

    @pl.loop(1, n)
    def _(i):
        stat_copy(me, lax.rem(me + n - i, n)).wait_recv()

    got = [stat_in[d] for d in range(n)]
    best = functools.reduce(jnp.maximum, got)
    got = [jnp.exp(g - best) for g in got]
    scale = 1.0 / functools.reduce(jnp.add, got)
    for d in range(n):
        spread[d * own : (d + 1) * own, :] = got[d] * scale
    share = jnp.transpose(spread[...])[:rows]

    @pl.loop(1, n)
    def _(i):
        part_copy(me, lax.rem(me + n - i, n)).wait_recv()

    for j in range(own):
        y = jnp.zeros((rows, vdim), jnp.float32)
        for d in range(n):
            at = d * own + j
            y = y + share[:, at : at + 1] * part_in[d, j].astype(jnp.float32)
        flat[me, :, j * vdim : (j + 1) * vdim] = y.astype(jnp.bfloat16)

    flat_copy(mirror, me, mirror).start()

    @pl.loop(1, half)
    def _(i):
        flat_copy(near(i), me, near(i)).start()

    def multiply(t):
        w_copy(t).wait()
        return lax.dot_general(
            flat[t], w[t], (((1,), (1,)), ((), ())), preferred_element_type=jnp.float32
        )

    total = multiply(me)
    flat_copy(me, mirror, mirror).wait_recv()

    @pl.loop(1, half)
    def _(i):
        flat_copy(near(i), mirror, far(i)).start()

    total = total + multiply(mirror)

    def step(at):
        def one(i, total):
            t = at(half - i)
            flat_copy(me, t, t).wait_recv()
            return total + multiply(t)

        return one

    total = lax.fori_loop(1, half, step(near), total)
    total = lax.fori_loop(1, half, step(far), total)
    group[my_head] = total.astype(jnp.bfloat16)

    def group_copy(to, slot):
        return pltpu.make_async_remote_copy(
            src_ref=group.at[slot],
            dst_ref=group.at[slot],
            send_sem=group_send.at[to],
            recv_sem=group_recv.at[slot],
            device_id={"head": to},
            device_id_type=MESH,
        )

    for j in range(1, n_head):
        group_copy(lax.rem(my_head + j, n_head), my_head).start()
    for j in range(1, n_head):
        group_copy(my_head, lax.rem(my_head + j, n_head)).wait_recv()
    out_ref[...] = group[...]

    @pl.loop(1, n)
    def _(i):
        t = lax.rem(me + i, n)
        stat_copy(t, me).wait_send()
        part_copy(t, me).wait_send()
        flat_copy(t, me, t).wait_send()

    for j in range(1, n_head):
        group_copy(lax.rem(my_head + j, n_head), my_head).wait_send()


def fused(n, n_head, queries, cache, block_ids, lengths, value_up, out_proj):
    rows, heads, width = queries.shape
    span = cache.shape[1]
    latent, vdim = value_up.shape[1:]
    columns = out_proj.shape[1]
    own = heads // n
    dma = pltpu.SemaphoreType.DMA
    any_space = pl.BlockSpec(memory_space=pl.ANY)
    groups = pl.pallas_call(
        functools.partial(kernel, n, n_head),
        out_shape=jax.ShapeDtypeStruct((n_head, rows, columns), jnp.bfloat16),
        in_specs=[
            pl.BlockSpec(memory_space=pltpu.SMEM),
            pl.BlockSpec(memory_space=pltpu.VMEM),
            any_space,
            any_space,
            any_space,
            any_space,
        ],
        out_specs=pl.BlockSpec(memory_space=pltpu.VMEM),
        scratch_shapes=[
            pltpu.VMEM((rows, heads, width), jnp.bfloat16),
            pltpu.VMEM((rows, width, span), jnp.bfloat16),
            pltpu.VMEM((heads, latent, vdim), jnp.bfloat16),
            pltpu.VMEM((n, columns, own * vdim), jnp.bfloat16),
            pltpu.VMEM((rows, heads, span), jnp.float32),
            pltpu.VMEM((latent // 128, rows * heads, 128), jnp.float32),
            pltpu.VMEM((n, own, 128), jnp.float32),
            pltpu.VMEM((n, own, 128), jnp.float32),
            pltpu.VMEM((heads, 128), jnp.float32),
            pltpu.VMEM((n, own, rows, vdim), jnp.bfloat16),
            pltpu.VMEM((n, own, rows, vdim), jnp.bfloat16),
            pltpu.VMEM((n, rows, own * vdim), jnp.bfloat16),
            pltpu.VMEM((n_head, rows, columns), jnp.bfloat16),
            dma((2, GROUPS)),
            dma((n,)),
            dma((n,)),
            dma((n,)),
            dma((n,)),
            dma((n,)),
            dma((n,)),
            dma((n,)),
            dma((n,)),
            dma((n_head,)),
            dma((n_head,)),
        ],
        compiler_params=pltpu.CompilerParams(
            collective_id=0, has_side_effects=True, vmem_limit_bytes=60 * 2**20
        ),
    )(
        lengths,
        block_ids,
        queries,
        jnp.transpose(cache, (0, 2, 1)),
        value_up,
        jnp.transpose(out_proj),
    )
    return jnp.sum(groups.astype(jnp.float32), axis=0).astype(jnp.bfloat16)


def spread_body(queries, cache, block_ids, lengths, value_up, out_proj):
    rows, span, width = cache.shape
    latent = value_up.shape[1]
    first = lax.axis_index("seq") * span
    position = first + jnp.arange(span, dtype=jnp.int32)
    chosen = jnp.any(block_ids[:, :, None] == (position // BLOCK)[None, None, :], axis=1)
    live = chosen & (position[None, :] < lengths[:, None])
    scores = (
        jnp.einsum("rhc,rsc->rhs", queries, cache, preferred_element_type=jnp.float32)
        * softmax_scale
    )
    masked = jnp.where(live[:, None, :], scores, -jnp.inf)
    local_top = jnp.max(masked, axis=-1)
    top = lax.pmax(local_top, "seq")
    expo = jnp.where(live[:, None, :], jnp.exp(masked - top[:, :, None]), jnp.float32(0.0))
    local_total = jnp.sum(expo, axis=-1)
    weights = expo.astype(jnp.bfloat16)
    summed = jnp.einsum(
        "rhs,rsc->rhc", weights, cache[:, :, :latent], preferred_element_type=jnp.float32
    )
    upward = value_up.astype(jnp.float32)
    total, summed_all = lax.psum((local_total, summed), "seq")
    context = summed_all / total[:, :, None]
    heads_out = jnp.einsum("rhc,hcv->rhv", context, upward, precision=lax.Precision.HIGHEST)
    flat = heads_out.astype(jnp.bfloat16).reshape(rows, -1)
    partial_out = jnp.dot(flat, out_proj, preferred_element_type=jnp.float32)
    return lax.psum(partial_out.astype(jnp.bfloat16), "head")


def body(n, n_head, *args):
    heads, span = args[0].shape[1], args[1].shape[1]
    if heads % n or n % 4 or span % BLOCK or span % 128:
        return spread_body(*args)
    return fused(n, n_head, *args)


def solution(mesh):
    return jax.shard_map(
        functools.partial(body, mesh.shape["seq"], mesh.shape["head"]),
        mesh=mesh,
        in_specs=(
            P(None, "head", None),
            P(None, "seq", None),
            P(),
            P(),
            P("head", None, None),
            P("head", "seq"),
        ),
        out_specs=P(None, "seq"),
        check_vma=False,
    )
```

```python
import functools

import jax
import jax.numpy as jnp
from jax import lax
from jax.experimental import pallas as pl
from jax.experimental.pallas import tpu as pltpu
from jax.sharding import PartitionSpec as P

BLOCK = 64
DEAD = -1e30
GROUPS = 4
MESH = pl.DeviceIdType.MESH


softmax_scale = 192.0 ** (-0.5)


def kernel(
    n,
    n_head,
    lengths_ref,
    ids_ref,
    q_hbm,
    k_hbm,
    v_hbm,
    w_hbm,
    out_ref,
    q,
    k,
    v,
    w,
    scores,
    summed,
    stat_out,
    stat_in,
    spread,
    part_out,
    part_in,
    flat,
    group,
    local_sem,
    v_sem,
    w_sem,
    stat_send,
    stat_recv,
    part_send,
    part_recv,
    flat_send,
    flat_recv,
    group_send,
    group_recv,
):
    rows, heads, width = q.shape
    span = k.shape[2]
    latent, vdim = v.shape[1:]
    own = heads // n
    tiles = latent // 128
    piece = own * vdim
    me = lax.axis_index("seq")
    my_head = lax.axis_index("head")
    half = n // 2
    pairs = half // 2
    some_heads = heads // 2
    side = me // half
    place = lax.rem(me, half)
    mirror = (1 - side) * half + place

    def near(i):
        return side * half + lax.rem(place + i, half)

    def first_copies(g):
        part = pl.ds(g * (rows // GROUPS), rows // GROUPS)
        return (
            pltpu.make_async_copy(q_hbm.at[part], q.at[part], local_sem.at[0, g]),
            pltpu.make_async_copy(k_hbm.at[part], k.at[part], local_sem.at[1, g]),
        )

    def v_copy(pair):
        part = pl.ds(pair * (2 * own), 2 * own)
        return pltpu.make_async_copy(v_hbm.at[part], v.at[part], v_sem.at[pair])

    def w_copy(at):
        part = pl.ds(pl.multiple_of(at * (half * piece), half * piece), half * piece)
        return pltpu.make_async_copy(w_hbm.at[:, part], w.at[at], w_sem.at[at])

    def pair_at(other, i):
        return other * pairs + lax.rem(place // 2 + 1 + i, pairs)

    for g in range(GROUPS):
        for copy in first_copies(g):
            copy.start()

    barrier = pltpu.get_barrier_semaphore()

    @pl.loop(1, n)
    def _(i):
        pl.semaphore_signal(
            barrier, inc=1, device_id={"seq": lax.rem(me + i, n)}, device_id_type=MESH
        )

    for j in range(1, n_head):
        pl.semaphore_signal(
            barrier, inc=1, device_id={"head": lax.rem(my_head + j, n_head)}, device_id_type=MESH
        )

    lane = lax.broadcasted_iota(jnp.int32, (rows, span), 1)
    line = lax.broadcasted_iota(jnp.int32, (rows, span), 0)
    first = me * span
    ids = ids_ref[...]
    chosen = jnp.zeros((rows, span), jnp.int32)
    for b in range(span // BLOCK):
        hit = jnp.max((ids == first // BLOCK + b).astype(jnp.int32), axis=1, keepdims=True)
        chosen = jnp.where(lane // BLOCK == b, hit, chosen)
    filled = jnp.zeros((rows, span), jnp.int32)
    for r in range(rows):
        filled = jnp.where(line == r, lengths_ref[r], filled)
    live = jnp.where(first + lane < filled, chosen, 0).astype(jnp.float32)

    def stat_copy(t):
        return pltpu.make_async_remote_copy(
            src_ref=stat_out.at[t],
            dst_ref=stat_in.at[me],
            send_sem=stat_send,
            recv_sem=stat_recv,
            device_id={"seq": t},
            device_id_type=MESH,
        )

    def part_copy(t):
        return pltpu.make_async_remote_copy(
            src_ref=part_out.at[t],
            dst_ref=part_in.at[me],
            send_sem=part_send,
            recv_sem=part_recv,
            device_id={"seq": t},
            device_id_type=MESH,
        )

    def flat_copy(t, slot, sem):
        return pltpu.make_async_remote_copy(
            src_ref=flat.at[slot],
            dst_ref=flat.at[slot],
            send_sem=flat_send,
            recv_sem=flat_recv.at[sem],
            device_id={"seq": t},
            device_id_type=MESH,
        )

    def several(ref, count, send_sem, recv_sem):
        part = ref.at[pl.ds(0, count)]
        return pltpu.make_async_remote_copy(
            src_ref=part,
            dst_ref=part,
            send_sem=send_sem,
            recv_sem=recv_sem,
            device_id={"seq": mirror},
            device_id_type=MESH,
        )

    def attend(other, opening):
        at = pl.multiple_of(other * some_heads, some_heads)
        for r in range(rows):
            if opening and r % (rows // GROUPS) == 0:
                for copy in first_copies(r // (rows // GROUPS)):
                    copy.wait()
            s = jnp.dot(
                q[r, pl.ds(at, some_heads), :], k[r], preferred_element_type=jnp.float32
            )
            scores[r] = jnp.where(live[r : r + 1] > 0.0, s * softmax_scale, DEAD)
        if opening:
            for i in range(pairs):
                v_copy(pair_at(other, i)).start()
            for i in range(pairs):
                v_copy(pair_at(1 - other, i)).start()
            w_copy(side).start()
            w_copy(1 - side).start()
        stats = jnp.zeros((some_heads, 128), jnp.float32)
        stat_lane = lax.broadcasted_iota(jnp.int32, (some_heads, 128), 1)
        for r in range(rows):
            s = scores[r]
            top = jnp.max(s, axis=1, keepdims=True)
            expo = jnp.where(live[r : r + 1] > 0.0, jnp.exp(s - top), 0.0)
            total = jnp.sum(expo, axis=1, keepdims=True)
            some = total > 0.0
            total = jnp.where(some, total, 1.0)
            stats = jnp.where(stat_lane == r, jnp.where(some, top + jnp.log(total), DEAD), stats)
            out = lax.dot_general(
                expo.astype(jnp.bfloat16),
                k[r, :latent, :],
                (((1,), (1,)), ((), ())),
                preferred_element_type=jnp.float32,
            )
            out = out * (1.0 / total)
            for c in range(tiles):
                summed[c, r * some_heads : (r + 1) * some_heads, :] = out[
                    :, c * 128 : (c + 1) * 128
                ]
        for t in range(half):
            stat_out[other * half + t] = stats[t * own : (t + 1) * own]

    def project(other, pair):
        v_copy(pair).wait()
        for j in range(2 * own):
            h = pair * (2 * own) + j
            x = jnp.concatenate(
                [
                    summed[c, pl.ds(h - other * some_heads, rows, stride=some_heads), :]
                    for c in range(tiles)
                ],
                axis=1,
            )
            y = jnp.dot(x.astype(jnp.bfloat16), v[h], preferred_element_type=jnp.float32)
            part_out[2 * pair + j // own, j % own] = y.astype(jnp.bfloat16)

    attend(1 - side, True)
    pl.semaphore_wait(barrier, n - 1 + n_head - 1)

    @pl.loop(0, pairs)
    def _(i):
        pair = pair_at(1 - side, i)
        project(1 - side, pair)
        for t in (2 * pair, 2 * pair + 1):
            part_copy(t).start()
            stat_copy(t).start()

    attend(side, False)

    @pl.loop(0, pairs - 1)
    def _(i):
        pair = pair_at(side, i)
        project(side, pair)
        for t in (2 * pair, 2 * pair + 1):
            part_copy(t).start()
            stat_copy(t).start()

    project(side, me // 2)
    beside = me // 2 * 2 + 1 - lax.rem(me, 2)
    part_copy(beside).start()
    stat_copy(beside).start()
    part_in[me] = part_out[me]
    stat_in[me] = stat_out[me]

    several(stat_in, n - 1, stat_send, stat_recv).wait_recv()
    got = [stat_in[d] for d in range(n)]
    best = functools.reduce(jnp.maximum, got)
    got = [jnp.exp(g - best) for g in got]
    scale = 1.0 / functools.reduce(jnp.add, got)
    for d in range(n):
        spread[d * own : (d + 1) * own, :] = got[d] * scale
    share = jnp.transpose(spread[...])[:rows]

    several(part_in, n - 1, part_send, part_recv).wait_recv()
    for j in range(own):
        y = jnp.zeros((rows, vdim), jnp.float32)
        for d in range(n):
            at = d * own + j
            y = y + share[:, at : at + 1] * part_in[d, j].astype(jnp.float32)
        flat[me, :, j * vdim : (j + 1) * vdim] = y.astype(jnp.bfloat16)

    flat_copy(mirror, me, 0).start()

    @pl.loop(1, half)
    def _(i):
        flat_copy(near(i), me, 1).start()

    flat_copy(me, mirror, 0).wait_recv()

    @pl.loop(1, half)
    def _(i):
        flat_copy(near(i), mirror, 2).start()

    def multiply(at):
        w_copy(at).wait()
        total = jnp.zeros((rows, w.shape[1]), jnp.float32)
        for t in range(half):
            total = total + lax.dot_general(
                flat[at * half + t],
                w[at, :, t * piece : (t + 1) * piece],
                (((1,), (1,)), ((), ())),
                preferred_element_type=jnp.float32,
            )
        return total

    several(flat, half - 1, flat_send, flat_recv.at[1]).wait_recv()
    total = multiply(side)
    several(flat, half - 1, flat_send, flat_recv.at[2]).wait_recv()
    total = total + multiply(1 - side)
    group[my_head] = total.astype(jnp.bfloat16)

    def group_copy(to, slot):
        return pltpu.make_async_remote_copy(
            src_ref=group.at[slot],
            dst_ref=group.at[slot],
            send_sem=group_send.at[to],
            recv_sem=group_recv.at[slot],
            device_id={"head": to},
            device_id_type=MESH,
        )

    for j in range(1, n_head):
        group_copy(lax.rem(my_head + j, n_head), my_head).start()
    for j in range(1, n_head):
        group_copy(my_head, lax.rem(my_head + j, n_head)).wait_recv()
    out_ref[...] = group[...]

    several(stat_out, n - 1, stat_send, stat_recv).wait_send()
    several(part_out, n - 1, part_send, part_recv).wait_send()
    several(flat, n - 1, flat_send, flat_recv.at[0]).wait_send()
    for j in range(1, n_head):
        group_copy(lax.rem(my_head + j, n_head), my_head).wait_send()


def fused(n, n_head, queries, cache, block_ids, lengths, value_up, out_proj):
    rows, heads, width = queries.shape
    span = cache.shape[1]
    latent, vdim = value_up.shape[1:]
    columns = out_proj.shape[1]
    own = heads // n
    half = n // 2
    dma = pltpu.SemaphoreType.DMA
    any_space = pl.BlockSpec(memory_space=pl.ANY)
    groups = pl.pallas_call(
        functools.partial(kernel, n, n_head),
        out_shape=jax.ShapeDtypeStruct((n_head, rows, columns), jnp.bfloat16),
        in_specs=[
            pl.BlockSpec(memory_space=pltpu.SMEM),
            pl.BlockSpec(memory_space=pltpu.VMEM),
            any_space,
            any_space,
            any_space,
            any_space,
        ],
        out_specs=pl.BlockSpec(memory_space=pltpu.VMEM),
        scratch_shapes=[
            pltpu.VMEM((rows, heads, width), jnp.bfloat16),
            pltpu.VMEM((rows, width, span), jnp.bfloat16),
            pltpu.VMEM((heads, latent, vdim), jnp.bfloat16),
            pltpu.VMEM((2, columns, half * own * vdim), jnp.bfloat16),
            pltpu.VMEM((rows, heads // 2, span), jnp.float32),
            pltpu.VMEM((latent // 128, rows * heads // 2, 128), jnp.float32),
            pltpu.VMEM((n, own, 128), jnp.float32),
            pltpu.VMEM((n, own, 128), jnp.float32),
            pltpu.VMEM((heads, 128), jnp.float32),
            pltpu.VMEM((n, own, rows, vdim), jnp.bfloat16),
            pltpu.VMEM((n, own, rows, vdim), jnp.bfloat16),
            pltpu.VMEM((n, rows, own * vdim), jnp.bfloat16),
            pltpu.VMEM((n_head, rows, columns), jnp.bfloat16),
            dma((2, GROUPS)),
            dma((half,)),
            dma((2,)),
            dma,
            dma,
            dma,
            dma,
            dma,
            dma((3,)),
            dma((n_head,)),
            dma((n_head,)),
        ],
        compiler_params=pltpu.CompilerParams(
            collective_id=0, has_side_effects=True, vmem_limit_bytes=60 * 2**20
        ),
    )(
        lengths,
        block_ids,
        queries,
        jnp.transpose(cache, (0, 2, 1)),
        value_up,
        jnp.transpose(out_proj),
    )
    return jnp.sum(groups.astype(jnp.float32), axis=0).astype(jnp.bfloat16)


def spread_body(queries, cache, block_ids, lengths, value_up, out_proj):
    rows, span, width = cache.shape
    latent = value_up.shape[1]
    first = lax.axis_index("seq") * span
    position = first + jnp.arange(span, dtype=jnp.int32)
    chosen = jnp.any(block_ids[:, :, None] == (position // BLOCK)[None, None, :], axis=1)
    live = chosen & (position[None, :] < lengths[:, None])
    scores = (
        jnp.einsum("rhc,rsc->rhs", queries, cache, preferred_element_type=jnp.float32)
        * softmax_scale
    )
    masked = jnp.where(live[:, None, :], scores, -jnp.inf)
    local_top = jnp.max(masked, axis=-1)
    top = lax.pmax(local_top, "seq")
    expo = jnp.where(live[:, None, :], jnp.exp(masked - top[:, :, None]), jnp.float32(0.0))
    local_total = jnp.sum(expo, axis=-1)
    weights = expo.astype(jnp.bfloat16)
    summed = jnp.einsum(
        "rhs,rsc->rhc", weights, cache[:, :, :latent], preferred_element_type=jnp.float32
    )
    upward = value_up.astype(jnp.float32)
    total, summed_all = lax.psum((local_total, summed), "seq")
    context = summed_all / total[:, :, None]
    heads_out = jnp.einsum("rhc,hcv->rhv", context, upward, precision=lax.Precision.HIGHEST)
    flat = heads_out.astype(jnp.bfloat16).reshape(rows, -1)
    partial_out = jnp.dot(flat, out_proj, preferred_element_type=jnp.float32)
    return lax.psum(partial_out.astype(jnp.bfloat16), "head")


def body(n, n_head, *args):
    heads, span = args[0].shape[1], args[1].shape[1]
    if heads % n or n % 4 or span % BLOCK or span % 128:
        return spread_body(*args)
    return fused(n, n_head, *args)


def solution(mesh):
    return jax.shard_map(
        functools.partial(body, mesh.shape["seq"], mesh.shape["head"]),
        mesh=mesh,
        in_specs=(
            P(None, "head", None),
            P(None, "seq", None),
            P(),
            P(),
            P("head", None, None),
            P("head", "seq"),
        ),
        out_specs=P(None, "seq"),
        check_vma=False,
    )
```

```python
import functools

import jax
import jax.numpy as jnp
from jax import lax
from jax.experimental import pallas as pl
from jax.experimental.pallas import tpu as pltpu
from jax.sharding import PartitionSpec as P

BLOCK = 64
DEAD = -1e30
GROUPS = 4
BATCH = 8
MESH = pl.DeviceIdType.MESH


softmax_scale = 192.0 ** (-0.5)


def kernel(
    n,
    n_head,
    lengths_hbm,
    ids_hbm,
    q_hbm,
    k_hbm,
    v_hbm,
    w_hbm,
    out_ref,
    lengths_ref,
    ids_ref,
    q,
    k,
    v,
    w,
    scores,
    summed,
    stat_out,
    stat_in,
    spread,
    part_out,
    part_in,
    flat,
    group,
    small_sem,
    local_sem,
    v_sem,
    w_sem,
    stat_send,
    stat_recv,
    part_send,
    part_recv,
    flat_send,
    flat_recv,
    group_send,
    group_recv,
):
    rows, heads, width = q.shape
    span = k.shape[2]
    latent, vdim = v.shape[1:]
    own = heads // n
    tiles = latent // 128
    piece = own * vdim
    me = lax.axis_index("seq")
    my_head = lax.axis_index("head")
    half = n // 2
    pairs = half // 2
    some_heads = heads // 2
    side = me // half
    place = lax.rem(me, half)
    mirror = (1 - side) * half + place

    def near(i):
        return side * half + lax.rem(place + i, half)

    def first_copies(g):
        part = pl.ds(g * (rows // GROUPS), rows // GROUPS)
        return (
            pltpu.make_async_copy(q_hbm.at[part], q.at[part], local_sem.at[0, g]),
            pltpu.make_async_copy(k_hbm.at[part], k.at[part], local_sem.at[1, g]),
        )

    def v_copy(pair):
        part = pl.ds(pair * (2 * own), 2 * own)
        return pltpu.make_async_copy(v_hbm.at[part], v.at[part], v_sem.at[pair])

    def w_copy(at):
        part = pl.ds(pl.multiple_of(at * (half * piece), half * piece), half * piece)
        return pltpu.make_async_copy(w_hbm.at[:, part], w.at[at], w_sem.at[at])

    def pair_at(other, i):
        return other * pairs + lax.rem(place // 2 + 1 + i, pairs)

    small_copies = (
        pltpu.make_async_copy(ids_hbm, ids_ref, small_sem.at[0]),
        pltpu.make_async_copy(lengths_hbm, lengths_ref, small_sem.at[1]),
    )
    for copy in small_copies:
        copy.start()
    for g in range(GROUPS):
        for copy in first_copies(g):
            copy.start()

    barrier = pltpu.get_barrier_semaphore()

    @pl.loop(1, n)
    def _(i):
        pl.semaphore_signal(
            barrier, inc=1, device_id={"seq": lax.rem(me + i, n)}, device_id_type=MESH
        )

    for j in range(1, n_head):
        pl.semaphore_signal(
            barrier, inc=1, device_id={"head": lax.rem(my_head + j, n_head)}, device_id_type=MESH
        )

    for copy in small_copies:
        copy.wait()
    lane = lax.broadcasted_iota(jnp.int32, (rows, span), 1)
    line = lax.broadcasted_iota(jnp.int32, (rows, span), 0)
    first = me * span
    ids = ids_ref[...]
    chosen = jnp.zeros((rows, span), jnp.int32)
    for b in range(span // BLOCK):
        hit = jnp.max((ids == first // BLOCK + b).astype(jnp.int32), axis=1, keepdims=True)
        chosen = jnp.where(lane // BLOCK == b, hit, chosen)
    filled = jnp.zeros((rows, span), jnp.int32)
    for r in range(rows):
        filled = jnp.where(line == r, lengths_ref[r], filled)
    live = jnp.where(first + lane < filled, chosen, 0).astype(jnp.float32)

    def stat_copy(t):
        return pltpu.make_async_remote_copy(
            src_ref=stat_out.at[t],
            dst_ref=stat_in.at[me],
            send_sem=stat_send,
            recv_sem=stat_recv,
            device_id={"seq": t},
            device_id_type=MESH,
        )

    def part_copy(t):
        return pltpu.make_async_remote_copy(
            src_ref=part_out.at[t],
            dst_ref=part_in.at[me],
            send_sem=part_send,
            recv_sem=part_recv,
            device_id={"seq": t},
            device_id_type=MESH,
        )

    def flat_copy(t, slot, sem):
        return pltpu.make_async_remote_copy(
            src_ref=flat.at[slot],
            dst_ref=flat.at[slot],
            send_sem=flat_send,
            recv_sem=flat_recv.at[sem],
            device_id={"seq": t},
            device_id_type=MESH,
        )

    def several(ref, count, send_sem, recv_sem):
        part = ref.at[pl.ds(0, count)]
        return pltpu.make_async_remote_copy(
            src_ref=part,
            dst_ref=part,
            send_sem=send_sem,
            recv_sem=recv_sem,
            device_id={"seq": mirror},
            device_id_type=MESH,
        )

    def attend(other, opening):
        at = pl.multiple_of(other * some_heads, some_heads)
        for r in range(rows):
            if opening and r % (rows // GROUPS) == 0:
                for copy in first_copies(r // (rows // GROUPS)):
                    copy.wait()
            s = jnp.dot(
                q[r, pl.ds(at, some_heads), :], k[r], preferred_element_type=jnp.float32
            )
            scores[r] = jnp.where(live[r : r + 1] > 0.0, s * softmax_scale, DEAD)
        if opening:
            for i in range(pairs):
                v_copy(pair_at(other, i)).start()
            for i in range(pairs):
                v_copy(pair_at(1 - other, i)).start()
            w_copy(side).start()
            w_copy(1 - side).start()
        stats = jnp.zeros((some_heads, 128), jnp.float32)
        stat_lane = lax.broadcasted_iota(jnp.int32, (some_heads, 128), 1)
        for r0 in range(0, rows, BATCH):
            s = scores[r0 : r0 + BATCH]
            top = jnp.max(s, axis=2, keepdims=True)
            expo = jnp.where(s > 0.5 * DEAD, jnp.exp(s - top), 0.0)
            total = jnp.sum(expo, axis=2, keepdims=True)
            some = total > 0.0
            total = jnp.where(some, total, 1.0)
            log_sum = jnp.where(some, top + jnp.log(total), DEAD)
            inverse = 1.0 / total
            weights = expo.astype(jnp.bfloat16)
            for i in range(BATCH):
                r = r0 + i
                stats = jnp.where(stat_lane == r, log_sum[i], stats)
                out = lax.dot_general(
                    weights[i],
                    k[r, :latent, :],
                    (((1,), (1,)), ((), ())),
                    preferred_element_type=jnp.float32,
                )
                out = out * inverse[i]
                for c in range(tiles):
                    summed[c, r * some_heads : (r + 1) * some_heads, :] = out[
                        :, c * 128 : (c + 1) * 128
                    ]
        for t in range(half):
            stat_out[other * half + t] = stats[t * own : (t + 1) * own]

    def project(other, pair):
        v_copy(pair).wait()
        first_head = pair * (2 * own)
        local_head = first_head - other * some_heads
        contexts = [
            jnp.concatenate(
                [
                    summed[c, pl.ds(local_head + j, rows, stride=some_heads), :]
                    for c in range(tiles)
                ],
                axis=1,
            ).astype(jnp.bfloat16)
            for j in range(2 * own)
        ]
        parts = [
            jnp.dot(x, v[first_head + j], preferred_element_type=jnp.float32)
            for j, x in enumerate(contexts)
        ]
        for j, y in enumerate(parts):
            part_out[2 * pair + j // own, j % own] = y.astype(jnp.bfloat16)

    attend(1 - side, True)
    pl.semaphore_wait(barrier, n - 1 + n_head - 1)

    @pl.loop(0, pairs)
    def _(i):
        pair = pair_at(1 - side, i)
        project(1 - side, pair)
        for t in (2 * pair, 2 * pair + 1):
            part_copy(t).start()
            stat_copy(t).start()

    attend(side, False)

    @pl.loop(0, pairs - 1)
    def _(i):
        pair = pair_at(side, i)
        project(side, pair)
        for t in (2 * pair, 2 * pair + 1):
            part_copy(t).start()
            stat_copy(t).start()

    project(side, me // 2)
    beside = me // 2 * 2 + 1 - lax.rem(me, 2)
    part_copy(beside).start()
    stat_copy(beside).start()
    part_in[me] = part_out[me]
    stat_in[me] = stat_out[me]

    several(stat_in, n - 1, stat_send, stat_recv).wait_recv()
    got = [stat_in[d] for d in range(n)]
    best = functools.reduce(jnp.maximum, got)
    got = [jnp.exp(g - best) for g in got]
    scale = 1.0 / functools.reduce(jnp.add, got)
    for d in range(n):
        spread[d * own : (d + 1) * own, :] = got[d] * scale
    share = jnp.transpose(spread[...])[:rows]

    several(part_in, n - 1, part_send, part_recv).wait_recv()
    for j in range(own):
        y = jnp.zeros((rows, vdim), jnp.float32)
        for d in range(n):
            at = d * own + j
            y = y + share[:, at : at + 1] * part_in[d, j].astype(jnp.float32)
        flat[me, :, j * vdim : (j + 1) * vdim] = y.astype(jnp.bfloat16)

    flat_copy(mirror, me, 0).start()

    @pl.loop(1, half)
    def _(i):
        flat_copy(near(i), me, 1).start()

    flat_copy(me, mirror, 0).wait_recv()

    @pl.loop(1, half)
    def _(i):
        flat_copy(near(i), mirror, 2).start()

    def multiply(at):
        w_copy(at).wait()
        total = jnp.zeros((rows, w.shape[1]), jnp.float32)
        for t in range(half):
            total = total + lax.dot_general(
                flat[at * half + t],
                w[at, :, t * piece : (t + 1) * piece],
                (((1,), (1,)), ((), ())),
                preferred_element_type=jnp.float32,
            )
        return total

    several(flat, half - 1, flat_send, flat_recv.at[1]).wait_recv()
    total = multiply(side)
    several(flat, half - 1, flat_send, flat_recv.at[2]).wait_recv()
    total = total + multiply(1 - side)
    group[my_head] = total.astype(jnp.bfloat16)

    def group_copy(to, slot):
        return pltpu.make_async_remote_copy(
            src_ref=group.at[slot],
            dst_ref=group.at[slot],
            send_sem=group_send.at[to],
            recv_sem=group_recv.at[slot],
            device_id={"head": to},
            device_id_type=MESH,
        )

    for j in range(1, n_head):
        group_copy(lax.rem(my_head + j, n_head), my_head).start()
    for j in range(1, n_head):
        group_copy(my_head, lax.rem(my_head + j, n_head)).wait_recv()
    out_ref[...] = group[...]

    several(stat_out, n - 1, stat_send, stat_recv).wait_send()
    several(part_out, n - 1, part_send, part_recv).wait_send()
    several(flat, n - 1, flat_send, flat_recv.at[0]).wait_send()
    for j in range(1, n_head):
        group_copy(lax.rem(my_head + j, n_head), my_head).wait_send()


def fused(n, n_head, queries, cache, block_ids, lengths, value_up, out_proj):
    rows, heads, width = queries.shape
    span = cache.shape[1]
    latent, vdim = value_up.shape[1:]
    columns = out_proj.shape[1]
    own = heads // n
    half = n // 2
    dma = pltpu.SemaphoreType.DMA
    in_hbm = pl.BlockSpec(memory_space=pltpu.HBM)
    groups = pl.pallas_call(
        functools.partial(kernel, n, n_head),
        out_shape=jax.ShapeDtypeStruct((n_head, rows, columns), jnp.bfloat16),
        in_specs=[in_hbm] * 6,
        out_specs=pl.BlockSpec(memory_space=pltpu.VMEM),
        scratch_shapes=[
            pltpu.SMEM(lengths.shape, jnp.int32),
            pltpu.VMEM(block_ids.shape, jnp.int32),
            pltpu.VMEM((rows, heads, width), jnp.bfloat16),
            pltpu.VMEM((rows, width, span), jnp.bfloat16),
            pltpu.VMEM((heads, latent, vdim), jnp.bfloat16),
            pltpu.VMEM((2, columns, half * own * vdim), jnp.bfloat16),
            pltpu.VMEM((rows, heads // 2, span), jnp.float32),
            pltpu.VMEM((latent // 128, rows * heads // 2, 128), jnp.float32),
            pltpu.VMEM((n, own, 128), jnp.float32),
            pltpu.VMEM((n, own, 128), jnp.float32),
            pltpu.VMEM((heads, 128), jnp.float32),
            pltpu.VMEM((n, own, rows, vdim), jnp.bfloat16),
            pltpu.VMEM((n, own, rows, vdim), jnp.bfloat16),
            pltpu.VMEM((n, rows, own * vdim), jnp.bfloat16),
            pltpu.VMEM((n_head, rows, columns), jnp.bfloat16),
            dma((2,)),
            dma((2, GROUPS)),
            dma((half,)),
            dma((2,)),
            dma,
            dma,
            dma,
            dma,
            dma,
            dma((3,)),
            dma((n_head,)),
            dma((n_head,)),
        ],
        compiler_params=pltpu.CompilerParams(
            collective_id=0, has_side_effects=True, vmem_limit_bytes=60 * 2**20
        ),
    )(
        lengths,
        block_ids,
        queries,
        jnp.transpose(cache, (0, 2, 1)),
        value_up,
        jnp.transpose(out_proj),
    )
    return jnp.sum(groups.astype(jnp.float32), axis=0).astype(jnp.bfloat16)


def spread_body(queries, cache, block_ids, lengths, value_up, out_proj):
    rows, span, width = cache.shape
    latent = value_up.shape[1]
    first = lax.axis_index("seq") * span
    position = first + jnp.arange(span, dtype=jnp.int32)
    chosen = jnp.any(block_ids[:, :, None] == (position // BLOCK)[None, None, :], axis=1)
    live = chosen & (position[None, :] < lengths[:, None])
    scores = (
        jnp.einsum("rhc,rsc->rhs", queries, cache, preferred_element_type=jnp.float32)
        * softmax_scale
    )
    masked = jnp.where(live[:, None, :], scores, -jnp.inf)
    local_top = jnp.max(masked, axis=-1)
    top = lax.pmax(local_top, "seq")
    expo = jnp.where(live[:, None, :], jnp.exp(masked - top[:, :, None]), jnp.float32(0.0))
    local_total = jnp.sum(expo, axis=-1)
    weights = expo.astype(jnp.bfloat16)
    summed = jnp.einsum(
        "rhs,rsc->rhc", weights, cache[:, :, :latent], preferred_element_type=jnp.float32
    )
    upward = value_up.astype(jnp.float32)
    total, summed_all = lax.psum((local_total, summed), "seq")
    context = summed_all / total[:, :, None]
    heads_out = jnp.einsum("rhc,hcv->rhv", context, upward, precision=lax.Precision.HIGHEST)
    flat = heads_out.astype(jnp.bfloat16).reshape(rows, -1)
    partial_out = jnp.dot(flat, out_proj, preferred_element_type=jnp.float32)
    return lax.psum(partial_out.astype(jnp.bfloat16), "head")


def body(n, n_head, *args):
    heads, span = args[0].shape[1], args[1].shape[1]
    if heads % n or n % 4 or span % BLOCK or span % 128:
        return spread_body(*args)
    return fused(n, n_head, *args)


def solution(mesh):
    return jax.shard_map(
        functools.partial(body, mesh.shape["seq"], mesh.shape["head"]),
        mesh=mesh,
        in_specs=(
            P(None, "head", None),
            P(None, "seq", None),
            P(),
            P(),
            P("head", None, None),
            P("head", "seq"),
        ),
        out_specs=P(None, "seq"),
        check_vma=False,
    )
```

```python
import functools

import jax
import jax.numpy as jnp
from jax import lax
from jax.experimental import pallas as pl
from jax.experimental.pallas import tpu as pltpu
from jax.sharding import PartitionSpec as P

BLOCK = 64
DEAD = -1e30
GROUPS = 4
BATCH = 8
MESH = pl.DeviceIdType.MESH


softmax_scale = 192.0 ** (-0.5)


def kernel(
    n,
    n_head,
    lengths_hbm,
    ids_hbm,
    q_hbm,
    k_hbm,
    v_hbm,
    w_hbm,
    out_ref,
    lengths_ref,
    ids_ref,
    q,
    k,
    v,
    w,
    scores,
    summed,
    stat_out,
    stat_in,
    spread,
    part_out,
    part_in,
    flat,
    group,
    small_sem,
    local_sem,
    v_sem,
    w_sem,
    stat_send,
    stat_recv,
    part_send,
    part_recv,
    flat_send,
    flat_recv,
    group_send,
    group_recv,
):
    rows, heads, width = q.shape
    span = k.shape[2]
    latent, vdim = v.shape[1:]
    own = heads // n
    tiles = latent // 128
    piece = own * vdim
    me = lax.axis_index("seq")
    my_head = lax.axis_index("head")
    half = n // 2
    some_heads = heads // 2
    side = me // half
    place = lax.rem(me, half)
    mirror = (1 - side) * half + place

    def near(i):
        return side * half + lax.rem(place + i, half)

    def first_copies(g):
        part = pl.ds(g * (rows // GROUPS), rows // GROUPS)
        return (
            pltpu.make_async_copy(q_hbm.at[part], q.at[part], local_sem.at[0, g]),
            pltpu.make_async_copy(k_hbm.at[part], k.at[part], local_sem.at[1, g]),
        )

    def v_copy(at):
        part = pl.ds(at * some_heads, some_heads)
        return pltpu.make_async_copy(v_hbm.at[part], v.at[part], v_sem.at[at])

    def w_copy(at):
        part = pl.ds(pl.multiple_of(at * (half * piece), half * piece), half * piece)
        return pltpu.make_async_copy(w_hbm.at[:, part], w.at[at], w_sem.at[at])

    small_copies = (
        pltpu.make_async_copy(ids_hbm, ids_ref, small_sem.at[0]),
        pltpu.make_async_copy(lengths_hbm, lengths_ref, small_sem.at[1]),
    )
    for copy in small_copies:
        copy.start()
    for g in range(GROUPS):
        for copy in first_copies(g):
            copy.start()

    barrier = pltpu.get_barrier_semaphore()

    @pl.loop(1, n)
    def _(i):
        pl.semaphore_signal(
            barrier, inc=1, device_id={"seq": lax.rem(me + i, n)}, device_id_type=MESH
        )

    for j in range(1, n_head):
        pl.semaphore_signal(
            barrier, inc=1, device_id={"head": lax.rem(my_head + j, n_head)}, device_id_type=MESH
        )

    for copy in small_copies:
        copy.wait()
    lane = lax.broadcasted_iota(jnp.int32, (rows, span), 1)
    line = lax.broadcasted_iota(jnp.int32, (rows, span), 0)
    first = me * span
    ids = ids_ref[...]
    chosen = jnp.zeros((rows, span), jnp.int32)
    for b in range(span // BLOCK):
        hit = jnp.max((ids == first // BLOCK + b).astype(jnp.int32), axis=1, keepdims=True)
        chosen = jnp.where(lane // BLOCK == b, hit, chosen)
    filled = jnp.zeros((rows, span), jnp.int32)
    for r in range(rows):
        filled = jnp.where(line == r, lengths_ref[r], filled)
    live = jnp.where(first + lane < filled, chosen, 0).astype(jnp.float32)

    def stat_copy(t):
        return pltpu.make_async_remote_copy(
            src_ref=stat_out.at[t],
            dst_ref=stat_in.at[me],
            send_sem=stat_send,
            recv_sem=stat_recv,
            device_id={"seq": t},
            device_id_type=MESH,
        )

    def part_copy(t):
        return pltpu.make_async_remote_copy(
            src_ref=part_out.at[t],
            dst_ref=part_in.at[me],
            send_sem=part_send,
            recv_sem=part_recv,
            device_id={"seq": t},
            device_id_type=MESH,
        )

    def flat_copy(t, slot, sem):
        return pltpu.make_async_remote_copy(
            src_ref=flat.at[slot],
            dst_ref=flat.at[slot],
            send_sem=flat_send,
            recv_sem=flat_recv.at[sem],
            device_id={"seq": t},
            device_id_type=MESH,
        )

    def several(ref, count, send_sem, recv_sem):
        part = ref.at[pl.ds(0, count)]
        return pltpu.make_async_remote_copy(
            src_ref=part,
            dst_ref=part,
            send_sem=send_sem,
            recv_sem=recv_sem,
            device_id={"seq": mirror},
            device_id_type=MESH,
        )

    def attend(other, opening):
        at = pl.multiple_of(other * some_heads, some_heads)
        for r in range(rows):
            if opening and r % (rows // GROUPS) == 0:
                for copy in first_copies(r // (rows // GROUPS)):
                    copy.wait()
            s = jnp.dot(
                q[r, pl.ds(at, some_heads), :], k[r], preferred_element_type=jnp.float32
            )
            scores[r] = jnp.where(live[r : r + 1] > 0.0, s * softmax_scale, DEAD)
        if opening:
            v_copy(other).start()
            v_copy(1 - other).start()
            w_copy(side).start()
            w_copy(1 - side).start()
        stats = jnp.zeros((some_heads, 128), jnp.float32)
        stat_lane = lax.broadcasted_iota(jnp.int32, (some_heads, 128), 1)
        for r0 in range(0, rows, BATCH):
            s = scores[r0 : r0 + BATCH]
            top = jnp.max(s, axis=2, keepdims=True)
            expo = jnp.where(s > 0.5 * DEAD, jnp.exp(s - top), 0.0)
            total = jnp.sum(expo, axis=2, keepdims=True)
            some = total > 0.0
            total = jnp.where(some, total, 1.0)
            log_sum = jnp.where(some, top + jnp.log(total), DEAD)
            inverse = 1.0 / total
            weights = expo.astype(jnp.bfloat16)
            for i in range(BATCH):
                r = r0 + i
                stats = jnp.where(stat_lane == r, log_sum[i], stats)
                out = lax.dot_general(
                    weights[i],
                    k[r, :latent, :],
                    (((1,), (1,)), ((), ())),
                    preferred_element_type=jnp.float32,
                )
                out = out * inverse[i]
                for c in range(tiles):
                    summed[c, r * some_heads : (r + 1) * some_heads, :] = out[
                        :, c * 128 : (c + 1) * 128
                    ]
        for t in range(half):
            stat_out[other * half + t] = stats[t * own : (t + 1) * own]

    def project(other):
        v_copy(other).wait()
        for j0 in range(0, some_heads, 2 * own):
            contexts = [
                jnp.concatenate(
                    [summed[c, pl.ds(j, rows, stride=some_heads), :] for c in range(tiles)],
                    axis=1,
                ).astype(jnp.bfloat16)
                for j in range(j0, j0 + 2 * own)
            ]
            parts = [
                jnp.dot(x, v[other * some_heads + j0 + j], preferred_element_type=jnp.float32)
                for j, x in enumerate(contexts)
            ]
            for j, y in enumerate(parts):
                h = j0 + j
                part_out[other * half + h // own, h % own] = y.astype(jnp.bfloat16)

    attend(1 - side, True)
    project(1 - side)
    pl.semaphore_wait(barrier, n - 1 + n_head - 1)

    @pl.loop(0, half)
    def _(i):
        t = (1 - side) * half + lax.rem(place + i, half)
        part_copy(t).start()
        stat_copy(t).start()

    attend(side, False)
    project(side)

    @pl.loop(1, half)
    def _(i):
        part_copy(near(i)).start()
        stat_copy(near(i)).start()

    part_in[me] = part_out[me]
    stat_in[me] = stat_out[me]

    several(stat_in, n - 1, stat_send, stat_recv).wait_recv()
    got = [stat_in[d] for d in range(n)]
    best = functools.reduce(jnp.maximum, got)
    got = [jnp.exp(g - best) for g in got]
    scale = 1.0 / functools.reduce(jnp.add, got)
    for d in range(n):
        spread[d * own : (d + 1) * own, :] = got[d] * scale
    share = jnp.transpose(spread[...])[:rows]

    several(part_in, n - 1, part_send, part_recv).wait_recv()
    for j in range(own):
        y = jnp.zeros((rows, vdim), jnp.float32)
        for d in range(n):
            at = d * own + j
            y = y + share[:, at : at + 1] * part_in[d, j].astype(jnp.float32)
        flat[me, :, j * vdim : (j + 1) * vdim] = y.astype(jnp.bfloat16)

    flat_copy(mirror, me, 0).start()

    @pl.loop(1, half)
    def _(i):
        flat_copy(near(i), me, 1).start()

    flat_copy(me, mirror, 0).wait_recv()

    @pl.loop(1, half)
    def _(i):
        flat_copy(near(i), mirror, 2).start()

    def multiply(at):
        w_copy(at).wait()
        total = jnp.zeros((rows, w.shape[1]), jnp.float32)
        for t in range(half):
            total = total + lax.dot_general(
                flat[at * half + t],
                w[at, :, t * piece : (t + 1) * piece],
                (((1,), (1,)), ((), ())),
                preferred_element_type=jnp.float32,
            )
        return total

    several(flat, half - 1, flat_send, flat_recv.at[1]).wait_recv()
    total = multiply(side)
    several(flat, half - 1, flat_send, flat_recv.at[2]).wait_recv()
    total = total + multiply(1 - side)
    group[my_head] = total.astype(jnp.bfloat16)

    def group_copy(to, slot):
        return pltpu.make_async_remote_copy(
            src_ref=group.at[slot],
            dst_ref=group.at[slot],
            send_sem=group_send.at[to],
            recv_sem=group_recv.at[slot],
            device_id={"head": to},
            device_id_type=MESH,
        )

    for j in range(1, n_head):
        group_copy(lax.rem(my_head + j, n_head), my_head).start()
    for j in range(1, n_head):
        group_copy(my_head, lax.rem(my_head + j, n_head)).wait_recv()
    out_ref[...] = group[...]

    several(stat_out, n - 1, stat_send, stat_recv).wait_send()
    several(part_out, n - 1, part_send, part_recv).wait_send()
    several(flat, n - 1, flat_send, flat_recv.at[0]).wait_send()
    for j in range(1, n_head):
        group_copy(lax.rem(my_head + j, n_head), my_head).wait_send()


def fused(n, n_head, queries, cache, block_ids, lengths, value_up, out_proj):
    rows, heads, width = queries.shape
    span = cache.shape[1]
    latent, vdim = value_up.shape[1:]
    columns = out_proj.shape[1]
    own = heads // n
    half = n // 2
    dma = pltpu.SemaphoreType.DMA
    in_hbm = pl.BlockSpec(memory_space=pltpu.HBM)
    groups = pl.pallas_call(
        functools.partial(kernel, n, n_head),
        out_shape=jax.ShapeDtypeStruct((n_head, rows, columns), jnp.bfloat16),
        in_specs=[in_hbm] * 6,
        out_specs=pl.BlockSpec(memory_space=pltpu.VMEM),
        scratch_shapes=[
            pltpu.SMEM(lengths.shape, jnp.int32),
            pltpu.VMEM(block_ids.shape, jnp.int32),
            pltpu.VMEM((rows, heads, width), jnp.bfloat16),
            pltpu.VMEM((rows, width, span), jnp.bfloat16),
            pltpu.VMEM((heads, latent, vdim), jnp.bfloat16),
            pltpu.VMEM((2, columns, half * own * vdim), jnp.bfloat16),
            pltpu.VMEM((rows, heads // 2, span), jnp.float32),
            pltpu.VMEM((latent // 128, rows * heads // 2, 128), jnp.float32),
            pltpu.VMEM((n, own, 128), jnp.float32),
            pltpu.VMEM((n, own, 128), jnp.float32),
            pltpu.VMEM((heads, 128), jnp.float32),
            pltpu.VMEM((n, own, rows, vdim), jnp.bfloat16),
            pltpu.VMEM((n, own, rows, vdim), jnp.bfloat16),
            pltpu.VMEM((n, rows, own * vdim), jnp.bfloat16),
            pltpu.VMEM((n_head, rows, columns), jnp.bfloat16),
            dma((2,)),
            dma((2, GROUPS)),
            dma((2,)),
            dma((2,)),
            dma,
            dma,
            dma,
            dma,
            dma,
            dma((3,)),
            dma((n_head,)),
            dma((n_head,)),
        ],
        compiler_params=pltpu.CompilerParams(
            collective_id=0, has_side_effects=True, vmem_limit_bytes=60 * 2**20
        ),
    )(
        lengths,
        block_ids,
        queries,
        jnp.transpose(cache, (0, 2, 1)),
        value_up,
        jnp.transpose(out_proj),
    )
    return jnp.sum(groups.astype(jnp.float32), axis=0).astype(jnp.bfloat16)


def spread_body(queries, cache, block_ids, lengths, value_up, out_proj):
    rows, span, width = cache.shape
    latent = value_up.shape[1]
    first = lax.axis_index("seq") * span
    position = first + jnp.arange(span, dtype=jnp.int32)
    chosen = jnp.any(block_ids[:, :, None] == (position // BLOCK)[None, None, :], axis=1)
    live = chosen & (position[None, :] < lengths[:, None])
    scores = (
        jnp.einsum("rhc,rsc->rhs", queries, cache, preferred_element_type=jnp.float32)
        * softmax_scale
    )
    masked = jnp.where(live[:, None, :], scores, -jnp.inf)
    local_top = jnp.max(masked, axis=-1)
    top = lax.pmax(local_top, "seq")
    expo = jnp.where(live[:, None, :], jnp.exp(masked - top[:, :, None]), jnp.float32(0.0))
    local_total = jnp.sum(expo, axis=-1)
    weights = expo.astype(jnp.bfloat16)
    summed = jnp.einsum(
        "rhs,rsc->rhc", weights, cache[:, :, :latent], preferred_element_type=jnp.float32
    )
    upward = value_up.astype(jnp.float32)
    total, summed_all = lax.psum((local_total, summed), "seq")
    context = summed_all / total[:, :, None]
    heads_out = jnp.einsum("rhc,hcv->rhv", context, upward, precision=lax.Precision.HIGHEST)
    flat = heads_out.astype(jnp.bfloat16).reshape(rows, -1)
    partial_out = jnp.dot(flat, out_proj, preferred_element_type=jnp.float32)
    return lax.psum(partial_out.astype(jnp.bfloat16), "head")


def body(n, n_head, *args):
    heads, span = args[0].shape[1], args[1].shape[1]
    if heads % n or n % 4 or span % BLOCK or span % 128:
        return spread_body(*args)
    return fused(n, n_head, *args)


def solution(mesh):
    return jax.shard_map(
        functools.partial(body, mesh.shape["seq"], mesh.shape["head"]),
        mesh=mesh,
        in_specs=(
            P(None, "head", None),
            P(None, "seq", None),
            P(),
            P(),
            P("head", None, None),
            P("head", "seq"),
        ),
        out_specs=P(None, "seq"),
        check_vma=False,
    )
```

```python
import functools

import jax
import jax.numpy as jnp
from jax import lax
from jax.experimental import pallas as pl
from jax.experimental.pallas import tpu as pltpu
from jax.sharding import PartitionSpec as P

BLOCK = 64
DEAD = -1e30
GROUPS = 4
BATCH = 8
MESH = pl.DeviceIdType.MESH


softmax_scale = 192.0 ** (-0.5)


def kernel(
    n,
    n_head,
    lengths_hbm,
    ids_hbm,
    q_hbm,
    k_hbm,
    v_hbm,
    w_hbm,
    out_ref,
    lengths_ref,
    ids_ref,
    q,
    k,
    v,
    w,
    scores,
    summed,
    stat_out,
    stat_in,
    spread,
    part_out,
    part_in,
    flat,
    group,
    small_sem,
    local_sem,
    v_sem,
    w_sem,
    stat_send,
    stat_recv,
    part_send,
    part_recv,
    flat_send,
    flat_recv,
    group_send,
    group_recv,
):
    rows, heads, width = q.shape
    span = k.shape[2]
    latent, vdim = v.shape[1:]
    own = heads // n
    tiles = latent // 128
    piece = own * vdim
    me = lax.axis_index("seq")
    my_head = lax.axis_index("head")
    half = n // 2
    pairs = half // 2
    some_heads = heads // 2
    side = me // half
    place = lax.rem(me, half)
    mirror = (1 - side) * half + place

    def near(i):
        return side * half + lax.rem(place + i, half)

    def first_copies(g):
        part = pl.ds(g * (rows // GROUPS), rows // GROUPS)
        return (
            pltpu.make_async_copy(q_hbm.at[part], q.at[part], local_sem.at[0, g]),
            pltpu.make_async_copy(k_hbm.at[part], k.at[part], local_sem.at[1, g]),
        )

    def v_copy(pair):
        part = pl.ds(pair * (2 * own), 2 * own)
        return pltpu.make_async_copy(v_hbm.at[part], v.at[part], v_sem.at[pair])

    def w_copy(at):
        part = pl.ds(pl.multiple_of(at * (half * piece), half * piece), half * piece)
        return pltpu.make_async_copy(w_hbm.at[:, part], w.at[at], w_sem.at[at])

    def pair_at(other, i):
        return other * pairs + lax.rem(place // 2 + 1 + i, pairs)

    small_copies = (
        pltpu.make_async_copy(ids_hbm, ids_ref, small_sem.at[0]),
        pltpu.make_async_copy(lengths_hbm, lengths_ref, small_sem.at[1]),
    )
    for copy in small_copies:
        copy.start()
    for g in range(GROUPS):
        for copy in first_copies(g):
            copy.start()

    barrier = pltpu.get_barrier_semaphore()

    @pl.loop(1, n)
    def _(i):
        pl.semaphore_signal(
            barrier, inc=1, device_id={"seq": lax.rem(me + i, n)}, device_id_type=MESH
        )

    for j in range(1, n_head):
        pl.semaphore_signal(
            barrier, inc=1, device_id={"head": lax.rem(my_head + j, n_head)}, device_id_type=MESH
        )

    for copy in small_copies:
        copy.wait()
    lane = lax.broadcasted_iota(jnp.int32, (rows, span), 1)
    line = lax.broadcasted_iota(jnp.int32, (rows, span), 0)
    first = me * span
    ids = ids_ref[...]
    chosen = jnp.zeros((rows, span), jnp.int32)
    for b in range(span // BLOCK):
        hit = jnp.max((ids == first // BLOCK + b).astype(jnp.int32), axis=1, keepdims=True)
        chosen = jnp.where(lane // BLOCK == b, hit, chosen)
    filled = jnp.zeros((rows, span), jnp.int32)
    for r in range(rows):
        filled = jnp.where(line == r, lengths_ref[r], filled)
    live = jnp.where(first + lane < filled, chosen, 0).astype(jnp.float32)

    def stat_copy(t):
        return pltpu.make_async_remote_copy(
            src_ref=stat_out.at[t],
            dst_ref=stat_in.at[me],
            send_sem=stat_send,
            recv_sem=stat_recv,
            device_id={"seq": t},
            device_id_type=MESH,
        )

    def part_copy(t):
        return pltpu.make_async_remote_copy(
            src_ref=part_out.at[t],
            dst_ref=part_in.at[me],
            send_sem=part_send,
            recv_sem=part_recv,
            device_id={"seq": t},
            device_id_type=MESH,
        )

    def flat_copy(t, slot, sem):
        return pltpu.make_async_remote_copy(
            src_ref=flat.at[slot],
            dst_ref=flat.at[slot],
            send_sem=flat_send,
            recv_sem=flat_recv.at[sem],
            device_id={"seq": t},
            device_id_type=MESH,
        )

    def several(ref, count, send_sem, recv_sem):
        part = ref.at[pl.ds(0, count)]
        return pltpu.make_async_remote_copy(
            src_ref=part,
            dst_ref=part,
            send_sem=send_sem,
            recv_sem=recv_sem,
            device_id={"seq": mirror},
            device_id_type=MESH,
        )

    def attend(other, opening):
        at = pl.multiple_of(other * some_heads, some_heads)
        for r in range(rows):
            if opening and r % (rows // GROUPS) == 0:
                g = r // (rows // GROUPS)
                for copy in first_copies(g):
                    copy.wait()
                if g == 0:
                    for i in range(pairs):
                        v_copy(pair_at(other, i)).start()
                if g == GROUPS - 1:
                    for i in range(pairs):
                        v_copy(pair_at(1 - other, i)).start()
            s = jnp.dot(
                q[r, pl.ds(at, some_heads), :], k[r], preferred_element_type=jnp.float32
            )
            scores[r] = jnp.where(live[r : r + 1] > 0.0, s * softmax_scale, DEAD)
        stats = jnp.zeros((some_heads, 128), jnp.float32)
        stat_lane = lax.broadcasted_iota(jnp.int32, (some_heads, 128), 1)
        for r0 in range(0, rows, BATCH):
            s = scores[r0 : r0 + BATCH]
            top = jnp.max(s, axis=2, keepdims=True)
            expo = jnp.where(s > 0.5 * DEAD, jnp.exp(s - top), 0.0)
            total = jnp.sum(expo, axis=2, keepdims=True)
            some = total > 0.0
            total = jnp.where(some, total, 1.0)
            log_sum = jnp.where(some, top + jnp.log(total), DEAD)
            inverse = 1.0 / total
            weights = expo.astype(jnp.bfloat16)
            for i in range(BATCH):
                r = r0 + i
                stats = jnp.where(stat_lane == r, log_sum[i], stats)
                out = lax.dot_general(
                    weights[i],
                    k[r, :latent, :],
                    (((1,), (1,)), ((), ())),
                    preferred_element_type=jnp.float32,
                )
                out = out * inverse[i]
                for c in range(tiles):
                    summed[c, r * some_heads : (r + 1) * some_heads, :] = out[
                        :, c * 128 : (c + 1) * 128
                    ]
        for t in range(half):
            stat_out[other * half + t] = stats[t * own : (t + 1) * own]

    def project(other, pair):
        v_copy(pair).wait()
        first_head = pair * (2 * own)
        local_head = first_head - other * some_heads
        contexts = [
            jnp.concatenate(
                [
                    summed[c, pl.ds(local_head + j, rows, stride=some_heads), :]
                    for c in range(tiles)
                ],
                axis=1,
            ).astype(jnp.bfloat16)
            for j in range(2 * own)
        ]
        parts = [
            jnp.dot(x, v[first_head + j], preferred_element_type=jnp.float32)
            for j, x in enumerate(contexts)
        ]
        for j, y in enumerate(parts):
            part_out[2 * pair + j // own, j % own] = y.astype(jnp.bfloat16)

    attend(1 - side, True)
    pl.semaphore_wait(barrier, n - 1 + n_head - 1)

    @pl.loop(0, pairs)
    def _(i):
        pair = pair_at(1 - side, i)
        project(1 - side, pair)
        for t in (2 * pair, 2 * pair + 1):
            part_copy(t).start()
            stat_copy(t).start()

    w_copy(side).start()
    w_copy(1 - side).start()
    attend(side, False)

    @pl.loop(0, pairs - 1)
    def _(i):
        pair = pair_at(side, i)
        project(side, pair)
        for t in (2 * pair, 2 * pair + 1):
            part_copy(t).start()
            stat_copy(t).start()

    project(side, me // 2)
    beside = me // 2 * 2 + 1 - lax.rem(me, 2)
    part_copy(beside).start()
    stat_copy(beside).start()
    part_in[me] = part_out[me]
    stat_in[me] = stat_out[me]

    several(stat_in, n - 1, stat_send, stat_recv).wait_recv()
    got = [stat_in[d] for d in range(n)]
    best = functools.reduce(jnp.maximum, got)
    got = [jnp.exp(g - best) for g in got]
    scale = 1.0 / functools.reduce(jnp.add, got)
    for d in range(n):
        spread[d * own : (d + 1) * own, :] = got[d] * scale
    share = jnp.transpose(spread[...])[:rows]

    several(part_in, n - 1, part_send, part_recv).wait_recv()
    for j in range(own):
        y = jnp.zeros((rows, vdim), jnp.float32)
        for d in range(n):
            at = d * own + j
            y = y + share[:, at : at + 1] * part_in[d, j].astype(jnp.float32)
        flat[me, :, j * vdim : (j + 1) * vdim] = y.astype(jnp.bfloat16)

    flat_copy(mirror, me, 0).start()

    @pl.loop(1, half)
    def _(i):
        flat_copy(near(i), me, 1).start()

    flat_copy(me, mirror, 0).wait_recv()

    @pl.loop(1, half)
    def _(i):
        flat_copy(near(i), mirror, 2).start()

    def multiply(at):
        w_copy(at).wait()
        total = jnp.zeros((rows, w.shape[1]), jnp.float32)
        for t in range(half):
            total = total + lax.dot_general(
                flat[at * half + t],
                w[at, :, t * piece : (t + 1) * piece],
                (((1,), (1,)), ((), ())),
                preferred_element_type=jnp.float32,
            )
        return total

    several(flat, half - 1, flat_send, flat_recv.at[1]).wait_recv()
    total = multiply(side)
    several(flat, half - 1, flat_send, flat_recv.at[2]).wait_recv()
    total = total + multiply(1 - side)
    group[my_head] = total.astype(jnp.bfloat16)

    def group_copy(to, slot):
        return pltpu.make_async_remote_copy(
            src_ref=group.at[slot],
            dst_ref=group.at[slot],
            send_sem=group_send.at[to],
            recv_sem=group_recv.at[slot],
            device_id={"head": to},
            device_id_type=MESH,
        )

    for j in range(1, n_head):
        group_copy(lax.rem(my_head + j, n_head), my_head).start()
    for j in range(1, n_head):
        group_copy(my_head, lax.rem(my_head + j, n_head)).wait_recv()
    out_ref[...] = group[...]

    several(stat_out, n - 1, stat_send, stat_recv).wait_send()
    several(part_out, n - 1, part_send, part_recv).wait_send()
    several(flat, n - 1, flat_send, flat_recv.at[0]).wait_send()
    for j in range(1, n_head):
        group_copy(lax.rem(my_head + j, n_head), my_head).wait_send()


def fused(n, n_head, queries, cache, block_ids, lengths, value_up, out_proj):
    rows, heads, width = queries.shape
    span = cache.shape[1]
    latent, vdim = value_up.shape[1:]
    columns = out_proj.shape[1]
    own = heads // n
    half = n // 2
    dma = pltpu.SemaphoreType.DMA
    in_hbm = pl.BlockSpec(memory_space=pltpu.HBM)
    groups = pl.pallas_call(
        functools.partial(kernel, n, n_head),
        out_shape=jax.ShapeDtypeStruct((n_head, rows, columns), jnp.bfloat16),
        in_specs=[in_hbm] * 6,
        out_specs=pl.BlockSpec(memory_space=pltpu.VMEM),
        scratch_shapes=[
            pltpu.SMEM(lengths.shape, jnp.int32),
            pltpu.VMEM(block_ids.shape, jnp.int32),
            pltpu.VMEM((rows, heads, width), jnp.bfloat16),
            pltpu.VMEM((rows, width, span), jnp.bfloat16),
            pltpu.VMEM((heads, latent, vdim), jnp.bfloat16),
            pltpu.VMEM((2, columns, half * own * vdim), jnp.bfloat16),
            pltpu.VMEM((rows, heads // 2, span), jnp.float32),
            pltpu.VMEM((latent // 128, rows * heads // 2, 128), jnp.float32),
            pltpu.VMEM((n, own, 128), jnp.float32),
            pltpu.VMEM((n, own, 128), jnp.float32),
            pltpu.VMEM((heads, 128), jnp.float32),
            pltpu.VMEM((n, own, rows, vdim), jnp.bfloat16),
            pltpu.VMEM((n, own, rows, vdim), jnp.bfloat16),
            pltpu.VMEM((n, rows, own * vdim), jnp.bfloat16),
            pltpu.VMEM((n_head, rows, columns), jnp.bfloat16),
            dma((2,)),
            dma((2, GROUPS)),
            dma((half,)),
            dma((2,)),
            dma,
            dma,
            dma,
            dma,
            dma,
            dma((3,)),
            dma((n_head,)),
            dma((n_head,)),
        ],
        compiler_params=pltpu.CompilerParams(
            collective_id=0, has_side_effects=True, vmem_limit_bytes=60 * 2**20
        ),
    )(
        lengths,
        block_ids,
        queries,
        jnp.transpose(cache, (0, 2, 1)),
        value_up,
        jnp.transpose(out_proj),
    )
    return jnp.sum(groups.astype(jnp.float32), axis=0).astype(jnp.bfloat16)


def spread_body(queries, cache, block_ids, lengths, value_up, out_proj):
    rows, span, width = cache.shape
    latent = value_up.shape[1]
    first = lax.axis_index("seq") * span
    position = first + jnp.arange(span, dtype=jnp.int32)
    chosen = jnp.any(block_ids[:, :, None] == (position // BLOCK)[None, None, :], axis=1)
    live = chosen & (position[None, :] < lengths[:, None])
    scores = (
        jnp.einsum("rhc,rsc->rhs", queries, cache, preferred_element_type=jnp.float32)
        * softmax_scale
    )
    masked = jnp.where(live[:, None, :], scores, -jnp.inf)
    local_top = jnp.max(masked, axis=-1)
    top = lax.pmax(local_top, "seq")
    expo = jnp.where(live[:, None, :], jnp.exp(masked - top[:, :, None]), jnp.float32(0.0))
    local_total = jnp.sum(expo, axis=-1)
    weights = expo.astype(jnp.bfloat16)
    summed = jnp.einsum(
        "rhs,rsc->rhc", weights, cache[:, :, :latent], preferred_element_type=jnp.float32
    )
    upward = value_up.astype(jnp.float32)
    total, summed_all = lax.psum((local_total, summed), "seq")
    context = summed_all / total[:, :, None]
    heads_out = jnp.einsum("rhc,hcv->rhv", context, upward, precision=lax.Precision.HIGHEST)
    flat = heads_out.astype(jnp.bfloat16).reshape(rows, -1)
    partial_out = jnp.dot(flat, out_proj, preferred_element_type=jnp.float32)
    return lax.psum(partial_out.astype(jnp.bfloat16), "head")


def body(n, n_head, *args):
    heads, span = args[0].shape[1], args[1].shape[1]
    if heads % n or n % 4 or span % BLOCK or span % 128:
        return spread_body(*args)
    return fused(n, n_head, *args)


def solution(mesh):
    return jax.shard_map(
        functools.partial(body, mesh.shape["seq"], mesh.shape["head"]),
        mesh=mesh,
        in_specs=(
            P(None, "head", None),
            P(None, "seq", None),
            P(),
            P(),
            P("head", None, None),
            P("head", "seq"),
        ),
        out_specs=P(None, "seq"),
        check_vma=False,
    )
```

```python
import functools

import jax
import jax.numpy as jnp
from jax import lax
from jax.experimental import pallas as pl
from jax.experimental.pallas import tpu as pltpu
from jax.sharding import PartitionSpec as P

BLOCK = 64
DEAD = -1e30
GROUPS = 4
BATCH = 8
MESH = pl.DeviceIdType.MESH


softmax_scale = 192.0 ** (-0.5)


def kernel(
    n,
    n_head,
    lengths_hbm,
    ids_hbm,
    q_hbm,
    k_hbm,
    v_hbm,
    w_hbm,
    out_ref,
    lengths_ref,
    ids_ref,
    q,
    k,
    v,
    w,
    scores,
    summed,
    stat_out,
    stat_in,
    spread,
    part_out,
    part_in,
    flat,
    group,
    small_sem,
    local_sem,
    v_sem,
    w_sem,
    stat_send,
    stat_recv,
    part_send,
    part_recv,
    flat_send,
    flat_recv,
    group_send,
    group_recv,
):
    rows, heads, width = q.shape
    span = k.shape[2]
    latent, vdim = v.shape[1:]
    own = heads // n
    tiles = latent // 128
    piece = own * vdim
    me = lax.axis_index("seq")
    my_head = lax.axis_index("head")
    half = n // 2
    pairs = half // 2
    some_heads = heads // 2
    side = me // half
    place = lax.rem(me, half)
    mirror = (1 - side) * half + place

    def near(i):
        return side * half + lax.rem(place + i, half)

    def first_copies(g):
        part = pl.ds(g * (rows // GROUPS), rows // GROUPS)
        far = half_heads(1 - side)
        return (
            pltpu.make_async_copy(q_hbm.at[part, far], q.at[part, far], local_sem.at[0, g]),
            pltpu.make_async_copy(k_hbm.at[part], k.at[part], local_sem.at[1, g]),
        )

    def half_heads(other):
        return pl.ds(pl.multiple_of(other * some_heads, some_heads), some_heads)

    def near_queries():
        part = half_heads(side)
        return pltpu.make_async_copy(q_hbm.at[:, part], q.at[:, part], small_sem.at[2])

    def v_copy(pair):
        part = pl.ds(pair * (2 * own), 2 * own)
        return pltpu.make_async_copy(v_hbm.at[part], v.at[part], v_sem.at[pair])

    def w_copy(at):
        part = pl.ds(pl.multiple_of(at * (half * piece), half * piece), half * piece)
        return pltpu.make_async_copy(w_hbm.at[:, part], w.at[at], w_sem.at[at])

    def pair_at(other, i):
        return other * pairs + lax.rem(place // 2 + 1 + i, pairs)

    small_copies = (
        pltpu.make_async_copy(ids_hbm, ids_ref, small_sem.at[0]),
        pltpu.make_async_copy(lengths_hbm, lengths_ref, small_sem.at[1]),
    )
    for copy in small_copies:
        copy.start()
    for g in range(GROUPS):
        for copy in first_copies(g):
            copy.start()

    barrier = pltpu.get_barrier_semaphore()

    @pl.loop(1, n)
    def _(i):
        pl.semaphore_signal(
            barrier, inc=1, device_id={"seq": lax.rem(me + i, n)}, device_id_type=MESH
        )

    for j in range(1, n_head):
        pl.semaphore_signal(
            barrier, inc=1, device_id={"head": lax.rem(my_head + j, n_head)}, device_id_type=MESH
        )

    for copy in small_copies:
        copy.wait()
    lane = lax.broadcasted_iota(jnp.int32, (rows, span), 1)
    line = lax.broadcasted_iota(jnp.int32, (rows, span), 0)
    first = me * span
    ids = ids_ref[...]
    chosen = jnp.zeros((rows, span), jnp.int32)
    for b in range(span // BLOCK):
        hit = jnp.max((ids == first // BLOCK + b).astype(jnp.int32), axis=1, keepdims=True)
        chosen = jnp.where(lane // BLOCK == b, hit, chosen)
    filled = jnp.zeros((rows, span), jnp.int32)
    for r in range(rows):
        filled = jnp.where(line == r, lengths_ref[r], filled)
    live = jnp.where(first + lane < filled, chosen, 0).astype(jnp.float32)

    def stat_copy(t):
        return pltpu.make_async_remote_copy(
            src_ref=stat_out.at[t],
            dst_ref=stat_in.at[me],
            send_sem=stat_send,
            recv_sem=stat_recv,
            device_id={"seq": t},
            device_id_type=MESH,
        )

    def part_copy(t):
        return pltpu.make_async_remote_copy(
            src_ref=part_out.at[t],
            dst_ref=part_in.at[me],
            send_sem=part_send,
            recv_sem=part_recv,
            device_id={"seq": t},
            device_id_type=MESH,
        )

    def flat_copy(t, slot, sem):
        return pltpu.make_async_remote_copy(
            src_ref=flat.at[slot],
            dst_ref=flat.at[slot],
            send_sem=flat_send,
            recv_sem=flat_recv.at[sem],
            device_id={"seq": t},
            device_id_type=MESH,
        )

    def several(ref, count, send_sem, recv_sem):
        part = ref.at[pl.ds(0, count)]
        return pltpu.make_async_remote_copy(
            src_ref=part,
            dst_ref=part,
            send_sem=send_sem,
            recv_sem=recv_sem,
            device_id={"seq": mirror},
            device_id_type=MESH,
        )

    def attend(other, opening):
        for r in range(rows):
            if opening and r % (rows // GROUPS) == 0:
                g = r // (rows // GROUPS)
                for copy in first_copies(g):
                    copy.wait()
                if g == 0:
                    for i in range(pairs):
                        v_copy(pair_at(other, i)).start()
                if g == GROUPS - 1:
                    near_queries().start()
                    for i in range(pairs):
                        v_copy(pair_at(1 - other, i)).start()
            s = jnp.dot(
                q[r, half_heads(other), :], k[r], preferred_element_type=jnp.float32
            )
            scores[r] = jnp.where(live[r : r + 1] > 0.0, s * softmax_scale, DEAD)
        stats = jnp.zeros((some_heads, 128), jnp.float32)
        stat_lane = lax.broadcasted_iota(jnp.int32, (some_heads, 128), 1)
        for r0 in range(0, rows, BATCH):
            s = scores[r0 : r0 + BATCH]
            top = jnp.max(s, axis=2, keepdims=True)
            expo = jnp.where(s > 0.5 * DEAD, jnp.exp(s - top), 0.0)
            total = jnp.sum(expo, axis=2, keepdims=True)
            some = total > 0.0
            total = jnp.where(some, total, 1.0)
            log_sum = jnp.where(some, top + jnp.log(total), DEAD)
            inverse = 1.0 / total
            weights = expo.astype(jnp.bfloat16)
            for i in range(BATCH):
                r = r0 + i
                stats = jnp.where(stat_lane == r, log_sum[i], stats)
                out = lax.dot_general(
                    weights[i],
                    k[r, :latent, :],
                    (((1,), (1,)), ((), ())),
                    preferred_element_type=jnp.float32,
                )
                out = out * inverse[i]
                for c in range(tiles):
                    summed[c, r * some_heads : (r + 1) * some_heads, :] = out[
                        :, c * 128 : (c + 1) * 128
                    ]
        for t in range(half):
            stat_out[other * half + t] = stats[t * own : (t + 1) * own]

    def project(other, first_head, count):
        local_head = first_head - other * some_heads
        contexts = [
            jnp.concatenate(
                [
                    summed[c, pl.ds(local_head + j, rows, stride=some_heads), :]
                    for c in range(tiles)
                ],
                axis=1,
            ).astype(jnp.bfloat16)
            for j in range(count)
        ]
        parts = [
            jnp.dot(x, v[first_head + j], preferred_element_type=jnp.float32)
            for j, x in enumerate(contexts)
        ]
        for j, y in enumerate(parts):
            part_out[first_head // own + j // own, j % own] = y.astype(jnp.bfloat16)

    attend(1 - side, True)
    pl.semaphore_wait(barrier, n - 1 + n_head - 1)

    @pl.loop(0, pairs)
    def _(i):
        pair = pair_at(1 - side, i)
        v_copy(pair).wait()
        project(1 - side, 2 * pair * own, 2 * own)
        for t in (2 * pair, 2 * pair + 1):
            part_copy(t).start()
            stat_copy(t).start()

    w_copy(side).start()
    w_copy(1 - side).start()
    near_queries().wait()
    attend(side, False)

    @pl.loop(0, pairs - 1)
    def _(i):
        pair = pair_at(side, i)
        v_copy(pair).wait()
        project(side, 2 * pair * own, 2 * own)
        for t in (2 * pair, 2 * pair + 1):
            part_copy(t).start()
            stat_copy(t).start()

    beside = me // 2 * 2 + 1 - lax.rem(me, 2)
    v_copy(me // 2).wait()
    project(side, beside * own, own)
    part_copy(beside).start()
    stat_copy(beside).start()
    project(side, me * own, own)
    part_in[me] = part_out[me]
    stat_in[me] = stat_out[me]

    several(stat_in, n - 1, stat_send, stat_recv).wait_recv()
    got = [stat_in[d] for d in range(n)]
    best = functools.reduce(jnp.maximum, got)
    got = [jnp.exp(g - best) for g in got]
    scale = 1.0 / functools.reduce(jnp.add, got)
    for d in range(n):
        spread[d * own : (d + 1) * own, :] = got[d] * scale
    share = jnp.transpose(spread[...])[:rows]

    several(part_in, n - 1, part_send, part_recv).wait_recv()
    for j in range(own):
        y = jnp.zeros((rows, vdim), jnp.float32)
        for d in range(n):
            at = d * own + j
            y = y + share[:, at : at + 1] * part_in[d, j].astype(jnp.float32)
        flat[me, :, j * vdim : (j + 1) * vdim] = y.astype(jnp.bfloat16)

    flat_copy(mirror, me, 0).start()

    @pl.loop(1, half)
    def _(i):
        flat_copy(near(i), me, 1).start()

    flat_copy(me, mirror, 0).wait_recv()

    @pl.loop(1, half)
    def _(i):
        flat_copy(near(i), mirror, 2).start()

    def multiply(at):
        w_copy(at).wait()
        total = jnp.zeros((rows, w.shape[1]), jnp.float32)
        for t in range(half):
            total = total + lax.dot_general(
                flat[at * half + t],
                w[at, :, t * piece : (t + 1) * piece],
                (((1,), (1,)), ((), ())),
                preferred_element_type=jnp.float32,
            )
        return total

    several(flat, half - 1, flat_send, flat_recv.at[1]).wait_recv()
    total = multiply(side)
    several(flat, half - 1, flat_send, flat_recv.at[2]).wait_recv()
    total = total + multiply(1 - side)
    group[...] = total.astype(jnp.bfloat16)

    def group_copy(to, slot):
        return pltpu.make_async_remote_copy(
            src_ref=group,
            dst_ref=out_ref.at[slot],
            send_sem=group_send.at[to],
            recv_sem=group_recv.at[slot],
            device_id={"head": to},
            device_id_type=MESH,
        )

    for j in range(1, n_head):
        group_copy(lax.rem(my_head + j, n_head), my_head).start()
    own_group = pltpu.make_async_copy(group, out_ref.at[my_head], group_recv.at[my_head])
    own_group.start()

    several(stat_out, n - 1, stat_send, stat_recv).wait_send()
    several(part_out, n - 1, part_send, part_recv).wait_send()
    several(flat, n - 1, flat_send, flat_recv.at[0]).wait_send()
    for j in range(1, n_head):
        group_copy(lax.rem(my_head + j, n_head), my_head).wait_send()
    own_group.wait()
    for j in range(1, n_head):
        group_copy(my_head, lax.rem(my_head + j, n_head)).wait_recv()


def fused(n, n_head, queries, cache, block_ids, lengths, value_up, out_proj):
    rows, heads, width = queries.shape
    span = cache.shape[1]
    latent, vdim = value_up.shape[1:]
    columns = out_proj.shape[1]
    own = heads // n
    half = n // 2
    dma = pltpu.SemaphoreType.DMA
    in_hbm = pl.BlockSpec(memory_space=pltpu.HBM)
    groups = pl.pallas_call(
        functools.partial(kernel, n, n_head),
        out_shape=jax.ShapeDtypeStruct((n_head, rows, columns), jnp.bfloat16),
        in_specs=[in_hbm] * 6,
        out_specs=in_hbm,
        scratch_shapes=[
            pltpu.SMEM(lengths.shape, jnp.int32),
            pltpu.VMEM(block_ids.shape, jnp.int32),
            pltpu.VMEM((rows, heads, width), jnp.bfloat16),
            pltpu.VMEM((rows, width, span), jnp.bfloat16),
            pltpu.VMEM((heads, latent, vdim), jnp.bfloat16),
            pltpu.VMEM((2, columns, half * own * vdim), jnp.bfloat16),
            pltpu.VMEM((rows, heads // 2, span), jnp.float32),
            pltpu.VMEM((latent // 128, rows * heads // 2, 128), jnp.float32),
            pltpu.VMEM((n, own, 128), jnp.float32),
            pltpu.VMEM((n, own, 128), jnp.float32),
            pltpu.VMEM((heads, 128), jnp.float32),
            pltpu.VMEM((n, own, rows, vdim), jnp.bfloat16),
            pltpu.VMEM((n, own, rows, vdim), jnp.bfloat16),
            pltpu.VMEM((n, rows, own * vdim), jnp.bfloat16),
            pltpu.VMEM((rows, columns), jnp.bfloat16),
            dma((3,)),
            dma((2, GROUPS)),
            dma((half,)),
            dma((2,)),
            dma,
            dma,
            dma,
            dma,
            dma,
            dma((3,)),
            dma((n_head,)),
            dma((n_head,)),
        ],
        compiler_params=pltpu.CompilerParams(
            collective_id=0, has_side_effects=True, vmem_limit_bytes=60 * 2**20
        ),
    )(
        lengths,
        block_ids,
        queries,
        jnp.transpose(cache, (0, 2, 1)),
        value_up,
        jnp.transpose(out_proj),
    )
    return jnp.sum(groups.astype(jnp.float32), axis=0).astype(jnp.bfloat16)


def spread_body(queries, cache, block_ids, lengths, value_up, out_proj):
    rows, span, width = cache.shape
    latent = value_up.shape[1]
    first = lax.axis_index("seq") * span
    position = first + jnp.arange(span, dtype=jnp.int32)
    chosen = jnp.any(block_ids[:, :, None] == (position // BLOCK)[None, None, :], axis=1)
    live = chosen & (position[None, :] < lengths[:, None])
    scores = (
        jnp.einsum("rhc,rsc->rhs", queries, cache, preferred_element_type=jnp.float32)
        * softmax_scale
    )
    masked = jnp.where(live[:, None, :], scores, -jnp.inf)
    local_top = jnp.max(masked, axis=-1)
    top = lax.pmax(local_top, "seq")
    expo = jnp.where(live[:, None, :], jnp.exp(masked - top[:, :, None]), jnp.float32(0.0))
    local_total = jnp.sum(expo, axis=-1)
    weights = expo.astype(jnp.bfloat16)
    summed = jnp.einsum(
        "rhs,rsc->rhc", weights, cache[:, :, :latent], preferred_element_type=jnp.float32
    )
    upward = value_up.astype(jnp.float32)
    total, summed_all = lax.psum((local_total, summed), "seq")
    context = summed_all / total[:, :, None]
    heads_out = jnp.einsum("rhc,hcv->rhv", context, upward, precision=lax.Precision.HIGHEST)
    flat = heads_out.astype(jnp.bfloat16).reshape(rows, -1)
    partial_out = jnp.dot(flat, out_proj, preferred_element_type=jnp.float32)
    return lax.psum(partial_out.astype(jnp.bfloat16), "head")


def body(n, n_head, *args):
    heads, span = args[0].shape[1], args[1].shape[1]
    if heads % n or n % 4 or span % BLOCK or span % 128:
        return spread_body(*args)
    return fused(n, n_head, *args)


def solution(mesh):
    return jax.shard_map(
        functools.partial(body, mesh.shape["seq"], mesh.shape["head"]),
        mesh=mesh,
        in_specs=(
            P(None, "head", None),
            P(None, "seq", None),
            P(),
            P(),
            P("head", None, None),
            P("head", "seq"),
        ),
        out_specs=P(None, "seq"),
        check_vma=False,
    )
```

```python
import functools

import jax
import jax.numpy as jnp
from jax import lax
from jax.experimental import pallas as pl
from jax.experimental.pallas import tpu as pltpu
from jax.sharding import PartitionSpec as P

BLOCK = 64
DEAD = -1e30
GROUPS = 4
BATCH = 8
MESH = pl.DeviceIdType.MESH


softmax_scale = 192.0 ** (-0.5)


def kernel(
    n,
    n_head,
    lengths_hbm,
    ids_hbm,
    q_hbm,
    k_hbm,
    v_hbm,
    w_hbm,
    out_ref,
    lengths_ref,
    ids_ref,
    q,
    k,
    v,
    w,
    scores,
    summed,
    stat_out,
    stat_in,
    spread,
    part_out,
    part_in,
    flat,
    group,
    small_sem,
    local_sem,
    v_sem,
    w_sem,
    stat_send,
    stat_recv,
    part_send,
    part_recv,
    flat_send,
    flat_recv,
    group_send,
    group_recv,
):
    rows, heads, width = q.shape
    span = k.shape[2]
    latent, vdim = v.shape[1:]
    own = heads // n
    tiles = latent // 128
    piece = own * vdim
    me = lax.axis_index("seq")
    my_head = lax.axis_index("head")
    half = n // 2
    pairs = half // 2
    some_heads = heads // 2
    side = me // half
    place = lax.rem(me, half)
    mirror = (1 - side) * half + place

    def near(i):
        return side * half + lax.rem(place + i, half)

    def first_copies(g):
        part = pl.ds(g * (rows // GROUPS), rows // GROUPS)
        far = half_heads(1 - side)
        return (
            pltpu.make_async_copy(q_hbm.at[part, far], q.at[part, far], local_sem.at[0, g]),
            pltpu.make_async_copy(k_hbm.at[part], k.at[part], local_sem.at[1, g]),
        )

    def half_heads(other):
        return pl.ds(pl.multiple_of(other * some_heads, some_heads), some_heads)

    def near_queries():
        part = half_heads(side)
        return pltpu.make_async_copy(q_hbm.at[:, part], q.at[:, part], small_sem.at[2])

    def v_copy(pair):
        part = pl.ds(pair * (2 * own), 2 * own)
        return pltpu.make_async_copy(v_hbm.at[part], v.at[part], v_sem.at[pair])

    def w_copy(at):
        part = pl.ds(pl.multiple_of(at * (half * piece), half * piece), half * piece)
        return pltpu.make_async_copy(w_hbm.at[:, part], w.at[at], w_sem.at[at])

    def pair_at(other, i):
        return other * pairs + lax.rem(place // 2 + 1 + i, pairs)

    small_copies = (
        pltpu.make_async_copy(ids_hbm, ids_ref, small_sem.at[0]),
        pltpu.make_async_copy(lengths_hbm, lengths_ref, small_sem.at[1]),
    )
    for copy in small_copies:
        copy.start()
    for g in range(GROUPS):
        for copy in first_copies(g):
            copy.start()

    barrier = pltpu.get_barrier_semaphore()

    @pl.loop(1, n)
    def _(i):
        pl.semaphore_signal(
            barrier, inc=1, device_id={"seq": lax.rem(me + i, n)}, device_id_type=MESH
        )

    for j in range(1, n_head):
        pl.semaphore_signal(
            barrier, inc=1, device_id={"head": lax.rem(my_head + j, n_head)}, device_id_type=MESH
        )

    for copy in small_copies:
        copy.wait()
    lane = lax.broadcasted_iota(jnp.int32, (rows, span), 1)
    line = lax.broadcasted_iota(jnp.int32, (rows, span), 0)
    first = me * span
    ids = ids_ref[...]
    chosen = jnp.zeros((rows, span), jnp.int32)
    for b in range(span // BLOCK):
        hit = jnp.max((ids == first // BLOCK + b).astype(jnp.int32), axis=1, keepdims=True)
        chosen = jnp.where(lane // BLOCK == b, hit, chosen)
    filled = jnp.zeros((rows, span), jnp.int32)
    for r in range(rows):
        filled = jnp.where(line == r, lengths_ref[r], filled)
    live = jnp.where(first + lane < filled, chosen, 0).astype(jnp.float32)

    def stat_copy(t):
        return pltpu.make_async_remote_copy(
            src_ref=stat_out.at[t],
            dst_ref=stat_in.at[me],
            send_sem=stat_send,
            recv_sem=stat_recv,
            device_id={"seq": t},
            device_id_type=MESH,
        )

    def part_copy(t):
        return pltpu.make_async_remote_copy(
            src_ref=part_out.at[t],
            dst_ref=part_in.at[me],
            send_sem=part_send,
            recv_sem=part_recv,
            device_id={"seq": t},
            device_id_type=MESH,
        )

    def flat_copy(t, slot, sem):
        return pltpu.make_async_remote_copy(
            src_ref=flat.at[slot],
            dst_ref=flat.at[slot],
            send_sem=flat_send,
            recv_sem=flat_recv.at[sem],
            device_id={"seq": t},
            device_id_type=MESH,
        )

    def several(ref, count, send_sem, recv_sem):
        part = ref.at[pl.ds(0, count)]
        return pltpu.make_async_remote_copy(
            src_ref=part,
            dst_ref=part,
            send_sem=send_sem,
            recv_sem=recv_sem,
            device_id={"seq": mirror},
            device_id_type=MESH,
        )

    def attend(other, opening):
        for r in range(rows):
            if opening and r % (rows // GROUPS) == 0:
                g = r // (rows // GROUPS)
                for copy in first_copies(g):
                    copy.wait()
                if g == 0:
                    for i in range(pairs):
                        v_copy(pair_at(other, i)).start()
                if g == GROUPS - 1:
                    near_queries().start()
                    for i in range(pairs):
                        v_copy(pair_at(1 - other, i)).start()
            s = jnp.dot(
                q[r, half_heads(other), :], k[r], preferred_element_type=jnp.float32
            )
            scores[r] = jnp.where(live[r : r + 1] > 0.0, s * softmax_scale, DEAD)
        stats = jnp.zeros((some_heads, 128), jnp.float32)
        stat_lane = lax.broadcasted_iota(jnp.int32, (some_heads, 128), 1)
        for r0 in range(0, rows, BATCH):
            s = scores[r0 : r0 + BATCH]
            top = jnp.max(s, axis=2, keepdims=True)
            expo = jnp.where(s > 0.5 * DEAD, jnp.exp(s - top), 0.0)
            total = jnp.sum(expo, axis=2, keepdims=True)
            some = total > 0.0
            total = jnp.where(some, total, 1.0)
            log_sum = jnp.where(some, top + jnp.log(total), DEAD)
            inverse = 1.0 / total
            weights = expo.astype(jnp.bfloat16)
            for i in range(BATCH):
                r = r0 + i
                stats = jnp.where(stat_lane == r, log_sum[i], stats)
                out = lax.dot_general(
                    weights[i],
                    k[r, :latent, :],
                    (((1,), (1,)), ((), ())),
                    preferred_element_type=jnp.float32,
                )
                out = out * inverse[i]
                for c in range(tiles):
                    summed[c, r * some_heads : (r + 1) * some_heads, :] = out[
                        :, c * 128 : (c + 1) * 128
                    ]
        for t in range(half):
            stat_out[other * half + t] = stats[t * own : (t + 1) * own]

    def project(other, first_head, count):
        local_head = first_head - other * some_heads
        contexts = [
            jnp.concatenate(
                [
                    summed[c, pl.ds(local_head + j, rows, stride=some_heads), :]
                    for c in range(tiles)
                ],
                axis=1,
            ).astype(jnp.bfloat16)
            for j in range(count)
        ]
        parts = [
            jnp.dot(x, v[first_head + j], preferred_element_type=jnp.float32)
            for j, x in enumerate(contexts)
        ]
        for j, y in enumerate(parts):
            part_out[first_head // own + j // own, j % own] = y.astype(jnp.bfloat16)

    attend(1 - side, True)
    pl.semaphore_wait(barrier, n - 1 + n_head - 1)

    @pl.loop(0, pairs)
    def _(i):
        pair = pair_at(1 - side, i)
        v_copy(pair).wait()
        project(1 - side, 2 * pair * own, 2 * own)
        for t in (2 * pair, 2 * pair + 1):
            part_copy(t).start()
            stat_copy(t).start()

    w_copy(side).start()
    w_copy(1 - side).start()
    near_queries().wait()
    attend(side, False)

    @pl.loop(0, pairs - 1)
    def _(i):
        pair = pair_at(side, i)
        v_copy(pair).wait()
        project(side, 2 * pair * own, 2 * own)
        for t in (2 * pair, 2 * pair + 1):
            part_copy(t).start()
            stat_copy(t).start()

    beside = me // 2 * 2 + 1 - lax.rem(me, 2)
    v_copy(me // 2).wait()
    project(side, beside * own, own)
    part_copy(beside).start()
    stat_copy(beside).start()
    project(side, me * own, own)
    part_in[me] = part_out[me]
    stat_in[me] = stat_out[me]

    several(stat_in, n - 1, stat_send, stat_recv).wait_recv()
    got = [stat_in[d] for d in range(n)]
    best = functools.reduce(jnp.maximum, got)
    got = [jnp.exp(g - best) for g in got]
    scale = 1.0 / functools.reduce(jnp.add, got)
    for d in range(n):
        spread[d * own : (d + 1) * own, :] = got[d] * scale
    share = jnp.transpose(spread[...])[:rows]

    several(part_in, n - 1, part_send, part_recv).wait_recv()
    for j in range(own):
        y = jnp.zeros((rows, vdim), jnp.float32)
        for d in range(n):
            at = d * own + j
            y = y + share[:, at : at + 1] * part_in[d, j].astype(jnp.float32)
        flat[me, :, j * vdim : (j + 1) * vdim] = y.astype(jnp.bfloat16)

    flat_copy(mirror, me, 0).start()

    @pl.loop(1, half)
    def _(i):
        flat_copy(near(i), me, 1).start()

    flat_copy(me, mirror, 0).wait_recv()

    @pl.loop(1, half)
    def _(i):
        flat_copy(near(i), mirror, 2 + place).start()

    def multiply(at, t):
        part = t * piece if isinstance(t, int) else pl.multiple_of(t * piece, piece)
        return lax.dot_general(
            flat[at * half + t],
            w[at, :, pl.ds(part, piece)],
            (((1,), (1,)), ((), ())),
            preferred_element_type=jnp.float32,
        )

    several(flat, half - 1, flat_send, flat_recv.at[1]).wait_recv()
    w_copy(side).wait()
    w_copy(1 - side).wait()
    total = multiply(side, 0)
    for t in range(1, half):
        total = total + multiply(side, t)
    total = total + multiply(1 - side, place)

    def arrived(i, total):
        t = lax.rem(place + half - i, half)
        flat_copy(me, (1 - side) * half + t, 2 + t).wait_recv()
        return total + multiply(1 - side, t)

    total = lax.fori_loop(1, half, arrived, total)
    group[...] = total.astype(jnp.bfloat16)

    def group_copy(to, slot):
        return pltpu.make_async_remote_copy(
            src_ref=group,
            dst_ref=out_ref.at[slot],
            send_sem=group_send.at[to],
            recv_sem=group_recv.at[slot],
            device_id={"head": to},
            device_id_type=MESH,
        )

    for j in range(1, n_head):
        group_copy(lax.rem(my_head + j, n_head), my_head).start()
    own_group = pltpu.make_async_copy(group, out_ref.at[my_head], group_recv.at[my_head])
    own_group.start()

    several(stat_out, n - 1, stat_send, stat_recv).wait_send()
    several(part_out, n - 1, part_send, part_recv).wait_send()
    several(flat, n - 1, flat_send, flat_recv.at[0]).wait_send()
    for j in range(1, n_head):
        group_copy(lax.rem(my_head + j, n_head), my_head).wait_send()
    own_group.wait()
    for j in range(1, n_head):
        group_copy(my_head, lax.rem(my_head + j, n_head)).wait_recv()


def fused(n, n_head, queries, cache, block_ids, lengths, value_up, out_proj):
    rows, heads, width = queries.shape
    span = cache.shape[1]
    latent, vdim = value_up.shape[1:]
    columns = out_proj.shape[1]
    own = heads // n
    half = n // 2
    dma = pltpu.SemaphoreType.DMA
    in_hbm = pl.BlockSpec(memory_space=pltpu.HBM)
    groups = pl.pallas_call(
        functools.partial(kernel, n, n_head),
        out_shape=jax.ShapeDtypeStruct((n_head, rows, columns), jnp.bfloat16),
        in_specs=[in_hbm] * 6,
        out_specs=in_hbm,
        scratch_shapes=[
            pltpu.SMEM(lengths.shape, jnp.int32),
            pltpu.VMEM(block_ids.shape, jnp.int32),
            pltpu.VMEM((rows, heads, width), jnp.bfloat16),
            pltpu.VMEM((rows, width, span), jnp.bfloat16),
            pltpu.VMEM((heads, latent, vdim), jnp.bfloat16),
            pltpu.VMEM((2, columns, half * own * vdim), jnp.bfloat16),
            pltpu.VMEM((rows, heads // 2, span), jnp.float32),
            pltpu.VMEM((latent // 128, rows * heads // 2, 128), jnp.float32),
            pltpu.VMEM((n, own, 128), jnp.float32),
            pltpu.VMEM((n, own, 128), jnp.float32),
            pltpu.VMEM((heads, 128), jnp.float32),
            pltpu.VMEM((n, own, rows, vdim), jnp.bfloat16),
            pltpu.VMEM((n, own, rows, vdim), jnp.bfloat16),
            pltpu.VMEM((n, rows, own * vdim), jnp.bfloat16),
            pltpu.VMEM((rows, columns), jnp.bfloat16),
            dma((3,)),
            dma((2, GROUPS)),
            dma((half,)),
            dma((2,)),
            dma,
            dma,
            dma,
            dma,
            dma,
            dma((2 + half,)),
            dma((n_head,)),
            dma((n_head,)),
        ],
        compiler_params=pltpu.CompilerParams(
            collective_id=0, has_side_effects=True, vmem_limit_bytes=60 * 2**20
        ),
    )(
        lengths,
        block_ids,
        queries,
        jnp.transpose(cache, (0, 2, 1)),
        value_up,
        jnp.transpose(out_proj),
    )
    return jnp.sum(groups.astype(jnp.float32), axis=0).astype(jnp.bfloat16)


def spread_body(queries, cache, block_ids, lengths, value_up, out_proj):
    rows, span, width = cache.shape
    latent = value_up.shape[1]
    first = lax.axis_index("seq") * span
    position = first + jnp.arange(span, dtype=jnp.int32)
    chosen = jnp.any(block_ids[:, :, None] == (position // BLOCK)[None, None, :], axis=1)
    live = chosen & (position[None, :] < lengths[:, None])
    scores = (
        jnp.einsum("rhc,rsc->rhs", queries, cache, preferred_element_type=jnp.float32)
        * softmax_scale
    )
    masked = jnp.where(live[:, None, :], scores, -jnp.inf)
    local_top = jnp.max(masked, axis=-1)
    top = lax.pmax(local_top, "seq")
    expo = jnp.where(live[:, None, :], jnp.exp(masked - top[:, :, None]), jnp.float32(0.0))
    local_total = jnp.sum(expo, axis=-1)
    weights = expo.astype(jnp.bfloat16)
    summed = jnp.einsum(
        "rhs,rsc->rhc", weights, cache[:, :, :latent], preferred_element_type=jnp.float32
    )
    upward = value_up.astype(jnp.float32)
    total, summed_all = lax.psum((local_total, summed), "seq")
    context = summed_all / total[:, :, None]
    heads_out = jnp.einsum("rhc,hcv->rhv", context, upward, precision=lax.Precision.HIGHEST)
    flat = heads_out.astype(jnp.bfloat16).reshape(rows, -1)
    partial_out = jnp.dot(flat, out_proj, preferred_element_type=jnp.float32)
    return lax.psum(partial_out.astype(jnp.bfloat16), "head")


def body(n, n_head, *args):
    heads, span = args[0].shape[1], args[1].shape[1]
    if heads % n or n % 4 or span % BLOCK or span % 128:
        return spread_body(*args)
    return fused(n, n_head, *args)


def solution(mesh):
    return jax.shard_map(
        functools.partial(body, mesh.shape["seq"], mesh.shape["head"]),
        mesh=mesh,
        in_specs=(
            P(None, "head", None),
            P(None, "seq", None),
            P(),
            P(),
            P("head", None, None),
            P("head", "seq"),
        ),
        out_specs=P(None, "seq"),
        check_vma=False,
    )
```

```python
import functools

import jax
import jax.numpy as jnp
from jax import lax
from jax.experimental import pallas as pl
from jax.experimental.pallas import tpu as pltpu
from jax.sharding import PartitionSpec as P

BLOCK = 64
DEAD = -1e30
GROUPS = 4
BATCH = 8
MESH = pl.DeviceIdType.MESH


softmax_scale = 192.0 ** (-0.5)


def kernel(
    n,
    n_head,
    lengths_hbm,
    ids_hbm,
    q_hbm,
    k_hbm,
    v_hbm,
    w_hbm,
    out_ref,
    lengths_ref,
    ids_ref,
    q,
    k,
    v,
    w,
    scores,
    summed,
    stat_out,
    stat_in,
    spread,
    shares,
    part_out,
    part_in,
    flat,
    group,
    small_sem,
    local_sem,
    v_sem,
    w_sem,
    stat_send,
    stat_recv,
    part_send,
    part_recv,
    flat_send,
    flat_recv,
    group_send,
    group_recv,
):
    rows, heads, width = q.shape
    span = k.shape[2]
    latent, vdim = v.shape[1:]
    own = heads // n
    tiles = latent // 128
    piece = own * vdim
    me = lax.axis_index("seq")
    my_head = lax.axis_index("head")
    half = n // 2
    pairs = half // 2
    some_heads = heads // 2
    side = me // half
    place = lax.rem(me, half)
    mirror = (1 - side) * half + place

    def near(i):
        return side * half + lax.rem(place + i, half)

    def first_copies(g):
        part = pl.ds(g * (rows // GROUPS), rows // GROUPS)
        far = half_heads(1 - side)
        return (
            pltpu.make_async_copy(q_hbm.at[part, far], q.at[part, far], local_sem.at[0, g]),
            pltpu.make_async_copy(k_hbm.at[part], k.at[part], local_sem.at[1, g]),
        )

    def half_heads(other):
        return pl.ds(pl.multiple_of(other * some_heads, some_heads), some_heads)

    def near_queries():
        part = half_heads(side)
        return pltpu.make_async_copy(q_hbm.at[:, part], q.at[:, part], small_sem.at[2])

    def v_copy(pair):
        part = pl.ds(pair * (2 * own), 2 * own)
        return pltpu.make_async_copy(v_hbm.at[part], v.at[part], v_sem.at[pair])

    def w_copy(at):
        part = pl.ds(pl.multiple_of(at * (half * piece), half * piece), half * piece)
        return pltpu.make_async_copy(w_hbm.at[:, part], w.at[at], w_sem.at[at])

    def pair_at(other, i):
        return other * pairs + lax.rem(place // 2 + 1 + i, pairs)

    small_copies = (
        pltpu.make_async_copy(ids_hbm, ids_ref, small_sem.at[0]),
        pltpu.make_async_copy(lengths_hbm, lengths_ref, small_sem.at[1]),
    )
    for copy in small_copies:
        copy.start()
    for g in range(GROUPS):
        for copy in first_copies(g):
            copy.start()

    barrier = pltpu.get_barrier_semaphore()

    @pl.loop(1, n)
    def _(i):
        pl.semaphore_signal(
            barrier, inc=1, device_id={"seq": lax.rem(me + i, n)}, device_id_type=MESH
        )

    for j in range(1, n_head):
        pl.semaphore_signal(
            barrier, inc=1, device_id={"head": lax.rem(my_head + j, n_head)}, device_id_type=MESH
        )

    for copy in small_copies:
        copy.wait()
    lane = lax.broadcasted_iota(jnp.int32, (rows, span), 1)
    line = lax.broadcasted_iota(jnp.int32, (rows, span), 0)
    first = me * span
    ids = ids_ref[...]
    chosen = jnp.zeros((rows, span), jnp.int32)
    for b in range(span // BLOCK):
        hit = jnp.max((ids == first // BLOCK + b).astype(jnp.int32), axis=1, keepdims=True)
        chosen = jnp.where(lane // BLOCK == b, hit, chosen)
    filled = jnp.zeros((rows, span), jnp.int32)
    for r in range(rows):
        filled = jnp.where(line == r, lengths_ref[r], filled)
    live = jnp.where(first + lane < filled, chosen, 0).astype(jnp.float32)

    def stat_copy(t):
        return pltpu.make_async_remote_copy(
            src_ref=stat_out.at[t],
            dst_ref=stat_in.at[me],
            send_sem=stat_send,
            recv_sem=stat_recv,
            device_id={"seq": t},
            device_id_type=MESH,
        )

    def part_copy(t):
        return pltpu.make_async_remote_copy(
            src_ref=part_out.at[t],
            dst_ref=part_in.at[me],
            send_sem=part_send,
            recv_sem=part_recv,
            device_id={"seq": t},
            device_id_type=MESH,
        )

    def flat_copy(t, slot, sem):
        return pltpu.make_async_remote_copy(
            src_ref=flat.at[slot],
            dst_ref=flat.at[slot],
            send_sem=flat_send,
            recv_sem=flat_recv.at[sem],
            device_id={"seq": t},
            device_id_type=MESH,
        )

    def several(ref, count, send_sem, recv_sem):
        part = ref.at[pl.ds(0, count)]
        return pltpu.make_async_remote_copy(
            src_ref=part,
            dst_ref=part,
            send_sem=send_sem,
            recv_sem=recv_sem,
            device_id={"seq": mirror},
            device_id_type=MESH,
        )

    def attend(other, opening):
        for r in range(rows):
            if opening and r % (rows // GROUPS) == 0:
                g = r // (rows // GROUPS)
                for copy in first_copies(g):
                    copy.wait()
                if g == 0:
                    for i in range(pairs):
                        v_copy(pair_at(other, i)).start()
                if g == GROUPS - 1:
                    near_queries().start()
                    for i in range(pairs):
                        v_copy(pair_at(1 - other, i)).start()
            s = jnp.dot(
                q[r, half_heads(other), :], k[r], preferred_element_type=jnp.float32
            )
            scores[r] = jnp.where(live[r : r + 1] > 0.0, s * softmax_scale, DEAD)
        stats = jnp.zeros((some_heads, 128), jnp.float32)
        stat_lane = lax.broadcasted_iota(jnp.int32, (some_heads, 128), 1)
        for r0 in range(0, rows, BATCH):
            s = scores[r0 : r0 + BATCH]
            top = jnp.max(s, axis=2, keepdims=True)
            expo = jnp.where(s > 0.5 * DEAD, jnp.exp(s - top), 0.0)
            total = jnp.sum(expo, axis=2, keepdims=True)
            some = total > 0.0
            total = jnp.where(some, total, 1.0)
            log_sum = jnp.where(some, top + jnp.log(total), DEAD)
            inverse = 1.0 / total
            weights = expo.astype(jnp.bfloat16)
            for i in range(BATCH):
                r = r0 + i
                stats = jnp.where(stat_lane == r, log_sum[i], stats)
                out = lax.dot_general(
                    weights[i],
                    k[r, :latent, :],
                    (((1,), (1,)), ((), ())),
                    preferred_element_type=jnp.float32,
                )
                out = out * inverse[i]
                for c in range(tiles):
                    summed[c, r * some_heads : (r + 1) * some_heads, :] = out[
                        :, c * 128 : (c + 1) * 128
                    ]
        for t in range(half):
            stat_out[other * half + t] = stats[t * own : (t + 1) * own]

    def project(other, first_head, count):
        local_head = first_head - other * some_heads
        contexts = [
            jnp.concatenate(
                [
                    summed[c, pl.ds(local_head + j, rows, stride=some_heads), :]
                    for c in range(tiles)
                ],
                axis=1,
            ).astype(jnp.bfloat16)
            for j in range(count)
        ]
        parts = [
            jnp.dot(x, v[first_head + j], preferred_element_type=jnp.float32)
            for j, x in enumerate(contexts)
        ]
        for j, y in enumerate(parts):
            part_out[first_head // own + j // own, j % own] = y.astype(jnp.bfloat16)

    attend(1 - side, True)
    pl.semaphore_wait(barrier, n - 1 + n_head - 1)

    @pl.loop(0, half)
    def _(i):
        stat_copy((1 - side) * half + lax.rem(place + i, half)).start()

    @pl.loop(0, pairs)
    def _(i):
        pair = pair_at(1 - side, i)
        v_copy(pair).wait()
        project(1 - side, 2 * pair * own, 2 * own)
        for t in (2 * pair, 2 * pair + 1):
            part_copy(t).start()

    w_copy(side).start()
    w_copy(1 - side).start()
    near_queries().wait()
    attend(side, False)

    @pl.loop(1, half)
    def _(i):
        stat_copy(near(i)).start()

    @pl.loop(0, pairs - 1)
    def _(i):
        pair = pair_at(side, i)
        v_copy(pair).wait()
        project(side, 2 * pair * own, 2 * own)
        for t in (2 * pair, 2 * pair + 1):
            part_copy(t).start()

    beside = me // 2 * 2 + 1 - lax.rem(me, 2)
    v_copy(me // 2).wait()
    project(side, beside * own, own)
    part_copy(beside).start()
    project(side, me * own, own)
    part_in[me] = part_out[me]
    stat_in[me] = stat_out[me]

    several(stat_in, n - 1, stat_send, stat_recv).wait_recv()
    got = [stat_in[d] for d in range(n)]
    best = functools.reduce(jnp.maximum, got)
    got = [jnp.exp(g - best) for g in got]
    scale = 1.0 / functools.reduce(jnp.add, got)
    for d in range(n):
        spread[d * own : (d + 1) * own, :] = got[d] * scale
    share = jnp.transpose(spread[...])[:rows]
    for at in range(n * own):
        shares[at] = jnp.broadcast_to(share[:, at : at + 1], (rows, vdim))

    several(part_in, n - 1, part_send, part_recv).wait_recv()
    for j in range(own):
        y = jnp.zeros((rows, vdim), jnp.float32)
        for d in range(n):
            at = d * own + j
            y = y + shares[at] * part_in[d, j].astype(jnp.float32)
        flat[me, :, j * vdim : (j + 1) * vdim] = y.astype(jnp.bfloat16)

    flat_copy(mirror, me, 0).start()

    @pl.loop(1, half)
    def _(i):
        flat_copy(near(i), me, 1).start()

    flat_copy(me, mirror, 0).wait_recv()

    @pl.loop(1, half)
    def _(i):
        flat_copy(near(i), mirror, 2).start()

    def multiply(at):
        w_copy(at).wait()
        total = jnp.zeros((rows, w.shape[1]), jnp.float32)
        for t in range(half):
            total = total + lax.dot_general(
                flat[at * half + t],
                w[at, :, t * piece : (t + 1) * piece],
                (((1,), (1,)), ((), ())),
                preferred_element_type=jnp.float32,
            )
        return total

    several(flat, half - 1, flat_send, flat_recv.at[1]).wait_recv()
    total = multiply(side)
    several(flat, half - 1, flat_send, flat_recv.at[2]).wait_recv()
    total = total + multiply(1 - side)
    group[...] = total.astype(jnp.bfloat16)

    def group_copy(to, slot):
        return pltpu.make_async_remote_copy(
            src_ref=group,
            dst_ref=out_ref.at[slot],
            send_sem=group_send.at[to],
            recv_sem=group_recv.at[slot],
            device_id={"head": to},
            device_id_type=MESH,
        )

    for j in range(1, n_head):
        group_copy(lax.rem(my_head + j, n_head), my_head).start()
    own_group = pltpu.make_async_copy(group, out_ref.at[my_head], group_recv.at[my_head])
    own_group.start()

    several(stat_out, n - 1, stat_send, stat_recv).wait_send()
    several(part_out, n - 1, part_send, part_recv).wait_send()
    several(flat, n - 1, flat_send, flat_recv.at[0]).wait_send()
    for j in range(1, n_head):
        group_copy(lax.rem(my_head + j, n_head), my_head).wait_send()
    own_group.wait()
    for j in range(1, n_head):
        group_copy(my_head, lax.rem(my_head + j, n_head)).wait_recv()


def fused(n, n_head, queries, cache, block_ids, lengths, value_up, out_proj):
    rows, heads, width = queries.shape
    span = cache.shape[1]
    latent, vdim = value_up.shape[1:]
    columns = out_proj.shape[1]
    own = heads // n
    half = n // 2
    dma = pltpu.SemaphoreType.DMA
    in_hbm = pl.BlockSpec(memory_space=pltpu.HBM)
    groups = pl.pallas_call(
        functools.partial(kernel, n, n_head),
        out_shape=jax.ShapeDtypeStruct((n_head, rows, columns), jnp.bfloat16),
        in_specs=[in_hbm] * 6,
        out_specs=in_hbm,
        scratch_shapes=[
            pltpu.SMEM(lengths.shape, jnp.int32),
            pltpu.VMEM(block_ids.shape, jnp.int32),
            pltpu.VMEM((rows, heads, width), jnp.bfloat16),
            pltpu.VMEM((rows, width, span), jnp.bfloat16),
            pltpu.VMEM((heads, latent, vdim), jnp.bfloat16),
            pltpu.VMEM((2, columns, half * own * vdim), jnp.bfloat16),
            pltpu.VMEM((rows, heads // 2, span), jnp.float32),
            pltpu.VMEM((latent // 128, rows * heads // 2, 128), jnp.float32),
            pltpu.VMEM((n, own, 128), jnp.float32),
            pltpu.VMEM((n, own, 128), jnp.float32),
            pltpu.VMEM((heads, 128), jnp.float32),
            pltpu.VMEM((heads, rows, vdim), jnp.float32),
            pltpu.VMEM((n, own, rows, vdim), jnp.bfloat16),
            pltpu.VMEM((n, own, rows, vdim), jnp.bfloat16),
            pltpu.VMEM((n, rows, own * vdim), jnp.bfloat16),
            pltpu.VMEM((rows, columns), jnp.bfloat16),
            dma((3,)),
            dma((2, GROUPS)),
            dma((half,)),
            dma((2,)),
            dma,
            dma,
            dma,
            dma,
            dma,
            dma((3,)),
            dma((n_head,)),
            dma((n_head,)),
        ],
        compiler_params=pltpu.CompilerParams(
            collective_id=0, has_side_effects=True, vmem_limit_bytes=60 * 2**20
        ),
    )(
        lengths,
        block_ids,
        queries,
        jnp.transpose(cache, (0, 2, 1)),
        value_up,
        jnp.transpose(out_proj),
    )
    return jnp.sum(groups.astype(jnp.float32), axis=0).astype(jnp.bfloat16)


def spread_body(queries, cache, block_ids, lengths, value_up, out_proj):
    rows, span, width = cache.shape
    latent = value_up.shape[1]
    first = lax.axis_index("seq") * span
    position = first + jnp.arange(span, dtype=jnp.int32)
    chosen = jnp.any(block_ids[:, :, None] == (position // BLOCK)[None, None, :], axis=1)
    live = chosen & (position[None, :] < lengths[:, None])
    scores = (
        jnp.einsum("rhc,rsc->rhs", queries, cache, preferred_element_type=jnp.float32)
        * softmax_scale
    )
    masked = jnp.where(live[:, None, :], scores, -jnp.inf)
    local_top = jnp.max(masked, axis=-1)
    top = lax.pmax(local_top, "seq")
    expo = jnp.where(live[:, None, :], jnp.exp(masked - top[:, :, None]), jnp.float32(0.0))
    local_total = jnp.sum(expo, axis=-1)
    weights = expo.astype(jnp.bfloat16)
    summed = jnp.einsum(
        "rhs,rsc->rhc", weights, cache[:, :, :latent], preferred_element_type=jnp.float32
    )
    upward = value_up.astype(jnp.float32)
    total, summed_all = lax.psum((local_total, summed), "seq")
    context = summed_all / total[:, :, None]
    heads_out = jnp.einsum("rhc,hcv->rhv", context, upward, precision=lax.Precision.HIGHEST)
    flat = heads_out.astype(jnp.bfloat16).reshape(rows, -1)
    partial_out = jnp.dot(flat, out_proj, preferred_element_type=jnp.float32)
    return lax.psum(partial_out.astype(jnp.bfloat16), "head")


def body(n, n_head, *args):
    heads, span = args[0].shape[1], args[1].shape[1]
    if heads % n or n % 4 or span % BLOCK or span % 128:
        return spread_body(*args)
    return fused(n, n_head, *args)


def solution(mesh):
    return jax.shard_map(
        functools.partial(body, mesh.shape["seq"], mesh.shape["head"]),
        mesh=mesh,
        in_specs=(
            P(None, "head", None),
            P(None, "seq", None),
            P(),
            P(),
            P("head", None, None),
            P("head", "seq"),
        ),
        out_specs=P(None, "seq"),
        check_vma=False,
    )
```
